128 devices in a mesh: row: 16 (over z, x), col: 8 (over y, core).
Axes of the slice: x: 4, y: 4, z: 4, core: 2. Of those that a mesh axis runs over, the one named last changes fastest.
Arguments:
- source: bfloat16 [65536, 128], P(('row', 'col')), may hold values from -1.5 to 1.5
- target: bfloat16 [32768, 128], P(('col', 'row')), may hold values from -1.5 to 1.5
Outputs:
- source_potential: float32 [65536], P('row')
- target_potential: float32 [32768], P('col')
The draws below stay inside these ranges and needn't reach their ends.
All inputs are finite; a program needn't handle non-finite values.
Results may differ from the reference program's by a relative error of at most 0.0003.
Values may be sent and summed in bfloat16 or wider, within the bound.
A program may use at most 64 MiB of HBM per device.

```python
import math
import jax
import jax.numpy as jnp
from jax import lax

D = 128
ITERS = 3
SOURCES = 65536
TARGETS = 32768


def embed_rows(key, count):
    normal_key = jax.random.fold_in(key, 101)
    scale_key = jax.random.fold_in(key, 103)
    gauss = jnp.clip(jax.random.normal(normal_key, (count, D), jnp.float32), -6.0, 6.0)
    mixed = gauss
    scales = jnp.exp(jax.random.uniform(scale_key, (count,), jnp.float32, math.log(0.4), math.log(2.5)))
    return jnp.clip(mixed * scales[:, None] / math.sqrt(D), -1.5, 1.5)


def draw_target(key, part):
    points = embed_rows(key, TARGETS)
    return points.astype(jnp.bfloat16)


def draw_source(key, part):
    key = jax.random.fold_in(key, 5)
    points = embed_rows(key, SOURCES)
    return points.astype(jnp.bfloat16)


def setup_inputs(seed: int = 0) -> dict:
    key_of = jax.random.split(jax.random.key(seed), 3)
    source = draw_source(jax.random.fold_in(key_of[2], 71), 0)
    target = draw_target(jax.random.fold_in(key_of[2], 71), 0)
    return {"source": source, "target": target}


entropic = 0.02


def pair_cost(source_block, source_sq_block, target_block, target_sq_block):
    inner = lax.dot_general(source_block, target_block, (((1,), (1,)), ((), ())), preferred_element_type=jnp.float32)
    return source_sq_block[:, None] + target_sq_block[None, :] - 2.0 * inner


def reference(source, target):
    source_sq = jnp.sum(jnp.square(source.astype(jnp.float32)), axis=1)
    target_sq = jnp.sum(jnp.square(target.astype(jnp.float32)), axis=1)
    row_size = min(512, SOURCES)
    row_count = SOURCES // row_size
    col_size = min(512, TARGETS)
    col_count = TARGETS // col_size
    target_pot = jnp.zeros((TARGETS,), jnp.float32)
    source_pot = jnp.zeros((SOURCES,), jnp.float32)
    log_targets = jnp.log(jnp.float32(TARGETS))
    log_sources = jnp.log(jnp.float32(SOURCES))
    for sweep in range(ITERS):
        def source_rows(operands):
            block, block_sq = operands
            scores = (target_pot[None, :] - pair_cost(block, block_sq, target, target_sq)) / entropic
            highest = jnp.max(scores, axis=1)
            summed = jnp.sum(jnp.exp(scores - highest[:, None]), axis=1)
            return entropic * (log_targets - highest - jnp.log(summed))

        source_pot = lax.map(source_rows, (source.reshape(row_count, row_size, D), source_sq.reshape(row_count, row_size))).reshape(SOURCES)

        def target_cols(operands):
            block, block_sq = operands
            scores = (source_pot[:, None] - pair_cost(source, source_sq, block, block_sq)) / entropic
            highest = jnp.max(scores, axis=0)
            summed = jnp.sum(jnp.exp(scores - highest[None, :]), axis=0)
            return entropic * (log_sources - highest - jnp.log(summed))

        target_pot = lax.map(target_cols, (target.reshape(col_count, col_size, D), target_sq.reshape(col_count, col_size))).reshape(TARGETS)
    return source_pot, target_pot
```

```python
import functools
import math

import jax
import jax.numpy as jnp
from jax import lax
from jax.experimental import pallas as pl
from jax.experimental.pallas import tpu as pltpu
from jax.sharding import PartitionSpec as P

ITERS = 3
EPS = 0.02
LOG2E = 1.0 / math.log(2.0)
SCALE = 2.0 * LOG2E / EPS
BACK = EPS / LOG2E
F32 = jnp.float32
BF16 = jnp.bfloat16
MESH = pl.DeviceIdType.MESH


def log2(x):
    return jnp.log(x) * LOG2E


def split3(x):
    high = x.astype(BF16).astype(F32)
    mid = (x - high).astype(BF16).astype(F32)
    return high, mid, x - high - mid


def pick3(x, index):
    high, mid, low = split3(x)
    zero = jnp.zeros_like(high)
    return jnp.where(
        index == 0, high, jnp.where(index == 1, mid, jnp.where(index == 2, low, zero))
    ).astype(BF16)


def nt_dot(x, y):
    return lax.dot_general(x, y, (((1,), (1,)), ((), ())), preferred_element_type=F32)


def kernel(
    row_n, col_n, s_ref, t_ref, f_ref, g_ref,
    s_all, t_all, s_ext, t_ext, kept, z0, z1, part, col_high, s_sq, t_sq, from_col, from_row,
    s_send, s_recv, t_send, t_recv, col_send, col_recv, row_send, row_recv,
):
    own_s, depth = s_ref.shape
    own_t = t_ref.shape[0]
    ns, nt = own_s * col_n, own_t * row_n
    total_s, total_t = float(ns * row_n), float(nt * col_n)
    my_row, my_col = lax.axis_index("row"), lax.axis_index("col")
    col_peers = [lax.rem(my_col + k, col_n) for k in range(1, col_n)]
    row_peers = [lax.rem(my_row + k, row_n) for k in range(1, row_n)]

    barrier = pltpu.get_barrier_semaphore()
    for peer in col_peers:
        pl.semaphore_signal(barrier, inc=1, device_id={"col": peer}, device_id_type=MESH)
    for peer in row_peers:
        pl.semaphore_signal(barrier, inc=1, device_id={"row": peer}, device_id_type=MESH)
    pl.semaphore_wait(barrier, col_n + row_n - 2)

    s_rows = pl.ds(pl.multiple_of(my_col * own_s, own_s), own_s)
    t_rows = pl.ds(pl.multiple_of(my_row * own_t, own_t), own_t)
    gathers = []
    for k, peer in enumerate(row_peers):
        gathers.append(
            pltpu.make_async_remote_copy(
                t_ref, t_all.at[t_rows, :], t_send.at[k], t_recv.at[k],
                device_id={"row": peer}, device_id_type=MESH,
            )
        )
    for k, peer in enumerate(col_peers):
        gathers.append(
            pltpu.make_async_remote_copy(
                s_ref, s_all.at[s_rows, :], s_send.at[k], s_recv.at[k],
                device_id={"col": peer}, device_id_type=MESH,
            )
        )
    for copy in gathers:
        copy.start()
    s_all[s_rows, :] = s_ref[...]
    t_all[t_rows, :] = t_ref[...]
    for copy in gathers:
        copy.wait()

    chunk = min(512, own_s, own_t)
    lane = lax.broadcasted_iota(jnp.int32, (chunk, depth), 1)
    ones = jnp.where(lane < 3, 1.0, 0.0).astype(BF16)

    def s_prepare(i, _):
        rows = pl.ds(pl.multiple_of(i * chunk, chunk), chunk)
        x = s_all[rows, :].astype(F32)
        s_sq[:, rows] = jnp.sum(jnp.transpose(x * x), axis=0, keepdims=True)
        s_ext[rows, :] = ones
        return 0

    def t_prepare(i, _):
        rows = pl.ds(pl.multiple_of(i * chunk, chunk), chunk)
        x = t_all[rows, :].astype(F32)
        t_sq[:, rows] = jnp.sum(jnp.transpose(x * x), axis=0, keepdims=True)
        bias = jnp.sum(x * x, axis=1, keepdims=True) * -0.5
        t_ext[rows, :] = pick3(jnp.broadcast_to(bias, (chunk, depth)), lane)
        return 0

    lax.fori_loop(0, ns // chunk, s_prepare, 0)
    lax.fori_loop(0, nt // chunk, t_prepare, 0)

    def logs_pass(x_all, x_ext, w_all, w_ext, out, keep):
        nx, nw = x_all.shape[0], w_all.shape[0]
        width = z0.shape[1]
        tiles = nw // width
        step = min(512, nx)
        fine = min(64, step)

        def lanes(tile):
            return pl.ds(pl.multiple_of(tile * width, width), width)

        def scores(tile, q, z, highest):
            rows = pl.ds(q * step, step)
            at = lanes(tile)
            x = jnp.concatenate([x_all[rows, :], x_ext[rows, :]], axis=1)
            w = jnp.concatenate([w_all[at, :], w_ext[at, :]], axis=1)
            inner = nt_dot(x, w)
            z[rows, :] = inner
            return jnp.maximum(highest, jnp.max(inner.reshape(step // 8, 8, width), axis=0))

        def sums(tile, q, z, highest, summed):
            for j in range(q * step, (q + 1) * step, fine):
                rows = pl.ds(j, fine)
                shifted = z[rows, :].reshape(fine // 8, 8, width) - highest[None]
                terms = jnp.exp2(shifted * SCALE)
                if keep:
                    kept[rows, lanes(tile)] = terms.reshape(fine, width).astype(BF16)
                summed = summed + jnp.sum(terms, axis=0)
            return summed

        def settle(highest):
            return jnp.broadcast_to(jnp.max(highest, axis=0, keepdims=True), (8, width))

        low = jnp.full((8, width), -3e38, F32)

        def both(tile, z_now, highest, z_next):
            following = jnp.minimum(tile + 1, tiles - 1)
            new_high = low
            summed = jnp.zeros((8, width), F32)
            for q in range(nx // step):
                new_high = scores(following, q, z_next, new_high)
                summed = sums(tile, q, z_now, highest, summed)
            top = highest[0:1, :] * SCALE
            out[:, lanes(tile)] = top + log2(jnp.sum(summed, axis=0, keepdims=True))
            if keep:
                col_high[:, lanes(tile)] = top
            return settle(new_high)

        def pair(i, highest):
            highest = both(2 * i, z0, highest, z1)
            return both(2 * i + 1, z1, highest, z0)

        first = low
        for q in range(nx // step):
            first = scores(0, q, z0, first)
        lax.fori_loop(0, tiles // 2, pair, settle(first))

    def exchange(turn, sent, received, send, recv, axis, peers):
        copies = [
            pltpu.make_async_remote_copy(
                sent, received.at[turn, k], send.at[turn, k], recv.at[turn, k],
                device_id={axis: peer}, device_id_type=MESH,
            )
            for k, peer in enumerate(peers)
        ]
        for copy in copies:
            copy.start()
        for copy in copies:
            copy.wait()
        return [sent[...]] + [received[turn, k] for k in range(len(peers))]

    def over_col(turn):
        return exchange(turn, part.at[2 * turn], from_col, col_send, col_recv, "col", col_peers)

    def over_row(turn):
        return exchange(turn, part.at[2 * turn + 1], from_row, row_send, row_recv, "row", row_peers)

    def combined_logs(logs):
        highest = functools.reduce(jnp.maximum, logs)
        return highest + log2(sum(jnp.exp2(x - highest) for x in logs))

    logs_pass(t_all, t_ext, s_all, s_ext, part.at[0], False)
    f_first = math.log2(total_t) - combined_logs(over_col(0))
    f_ref[...] = f_first

    def s_bias(i, _):
        rows = pl.ds(pl.multiple_of(i * chunk, chunk), chunk)
        bias = jnp.transpose(jnp.broadcast_to(f_ref[:, rows] * (1.0 / SCALE), (depth, chunk)))
        s_ext[rows, :] = pick3(bias, lane)
        return 0

    def t_ones(i, _):
        t_ext[pl.ds(pl.multiple_of(i * chunk, chunk), chunk), :] = ones
        return 0

    lax.fori_loop(0, ns // chunk, s_bias, 0)
    lax.fori_loop(0, nt // chunk, t_ones, 0)
    logs_pass(s_all, s_ext, t_all, t_ext, part.at[1], True)
    g_first = math.log2(total_s) - combined_logs(over_row(0))
    g_ref[...] = g_first
    col_high[...] = jnp.exp2(g_first + col_high[...])

    block = min(512, ns, nt)

    def parts_of(x):
        return pick3(jnp.broadcast_to(x, (16, x.shape[1])), lax.broadcasted_iota(jnp.int32, (16, x.shape[1]), 0))

    def row_sums(x, out):
        lhs = parts_of(x)

        def one(i, _):
            rows = pl.ds(pl.multiple_of(i * block, block), block)
            out[:, rows] = jnp.sum(nt_dot(lhs, kept[rows, :]), axis=0, keepdims=True)
            return 0

        lax.fori_loop(0, ns // block, one, 0)

    def col_sums(x, out):
        lhs = parts_of(x)

        def one(i, _):
            at = pl.ds(pl.multiple_of(i * block, block), block)
            found = jnp.dot(lhs, kept[:, at], preferred_element_type=F32)
            out[:, at] = jnp.sum(found, axis=0, keepdims=True) * col_high[:, at]
            return 0

        lax.fori_loop(0, nt // block, one, 0)

    weight = col_high[...]
    for turn in range(1, ITERS):
        row_sums(weight, part.at[2 * turn])
        u = total_t / sum(over_col(turn))
        col_sums(u, part.at[2 * turn + 1])
        v = total_s / sum(over_row(turn))
        weight = col_high[...] * v
    f_ref[...] = BACK * (f_ref[...] + log2(u)) + s_sq[...]
    g_ref[...] = BACK * (g_ref[...] + log2(v)) + t_sq[...]


def on_device(row_n, col_n, source, target):
    own_s, depth = source.shape
    own_t = target.shape[0]
    ns, nt = own_s * col_n, own_t * row_n
    width = min(256, ns // 2, nt // 2)
    vmem = pl.BlockSpec(memory_space=pltpu.VMEM)
    dma = pltpu.SemaphoreType.DMA
    f, g = pl.pallas_call(
        functools.partial(kernel, row_n, col_n),
        out_shape=(jax.ShapeDtypeStruct((1, ns), F32), jax.ShapeDtypeStruct((1, nt), F32)),
        in_specs=[vmem, vmem],
        out_specs=(vmem, vmem),
        scratch_shapes=[
            pltpu.VMEM((ns, depth), BF16),
            pltpu.VMEM((nt, depth), BF16),
            pltpu.VMEM((ns, depth), BF16),
            pltpu.VMEM((nt, depth), BF16),
            pltpu.VMEM((ns, nt), BF16),
            pltpu.VMEM((max(ns, nt), width), F32),
            pltpu.VMEM((max(ns, nt), width), F32),
            pltpu.VMEM((2 * ITERS, 1, max(ns, nt)), F32),
            pltpu.VMEM((1, nt), F32),
            pltpu.VMEM((1, ns), F32),
            pltpu.VMEM((1, nt), F32),
            pltpu.VMEM((ITERS, col_n - 1, 1, ns), F32),
            pltpu.VMEM((ITERS, row_n - 1, 1, nt), F32),
            dma((col_n - 1,)),
            dma((col_n - 1,)),
            dma((row_n - 1,)),
            dma((row_n - 1,)),
            dma((ITERS, col_n - 1)),
            dma((ITERS, col_n - 1)),
            dma((ITERS, row_n - 1)),
            dma((ITERS, row_n - 1)),
        ],
        compiler_params=pltpu.CompilerParams(
            collective_id=0, has_side_effects=True, vmem_limit_bytes=60 << 20
        ),
        cost_estimate=pl.CostEstimate(
            flops=12 * ns * nt * depth, bytes_accessed=2 * (ns + nt) * depth, transcendentals=2 * ns * nt
        ),
    )(source, target)
    return f.reshape(ns), g.reshape(nt)


def solution(mesh):
    placed = (P(("row", "col"), None), P(("col", "row"), None))
    return jax.shard_map(
        functools.partial(on_device, mesh.shape["row"], mesh.shape["col"]),
        mesh=mesh,
        in_specs=placed,
        out_specs=(P("row"), P("col")),
        check_vma=False,
    )
```

```python
import functools
import math

import jax
import jax.numpy as jnp
from jax import lax
from jax.experimental import pallas as pl
from jax.experimental.pallas import tpu as pltpu
from jax.sharding import PartitionSpec as P

ITERS = 3
EPS = 0.02
LOG2E = 1.0 / math.log(2.0)
SCALE = 2.0 * LOG2E / EPS
BACK = EPS / LOG2E
FLOOR = 90.0
CEIL = 100.0
F32 = jnp.float32
BF16 = jnp.bfloat16
MESH = pl.DeviceIdType.MESH


def pair_cost(source_block, source_sq_block, target_block, target_sq_block):
    inner = lax.dot_general(
        source_block, target_block, (((1,), (1,)), ((), ())), preferred_element_type=jnp.float32
    )
    return source_sq_block[:, None] + target_sq_block[None, :] - 2.0 * inner


def combine_pairs(first, second):
    highest = jnp.maximum(first[0], second[0])
    summed = first[1] * jnp.exp(first[0] - highest) + second[1] * jnp.exp(second[0] - highest)
    return (highest, summed)


def source_partials(source_rows, source_sq, target_rows, target_sq, target_pot):
    total_rows = source_rows.shape[0]
    total_cols = target_rows.shape[0]
    row_size = min(512, total_rows)
    row_count = total_rows // row_size
    col_size = min(1024, total_cols)

    def source_one_block(operands):
        block, block_sq = operands
        highest = jnp.full((row_size,), -jnp.inf, jnp.float32)
        summed = jnp.zeros((row_size,), jnp.float32)
        for offset in range(0, total_cols, col_size):
            scores = (
                target_pot[offset : offset + col_size][None, :]
                - pair_cost(
                    block,
                    block_sq,
                    target_rows[offset : offset + col_size],
                    target_sq[offset : offset + col_size],
                )
            ) / EPS
            block_high = jnp.max(scores, axis=1)
            block_sum = jnp.sum(jnp.exp(scores - block_high[:, None]), axis=1)
            highest, summed = combine_pairs((highest, summed), (block_high, block_sum))
        return (highest, summed)

    highest, summed = lax.map(
        source_one_block,
        (
            source_rows.reshape(row_count, row_size, source_rows.shape[1]),
            source_sq.reshape(row_count, row_size),
        ),
    )
    return (highest.reshape(total_rows), summed.reshape(total_rows))


def target_partials(source_rows, source_sq, target_rows, target_sq, source_pot):
    total_rows = source_rows.shape[0]
    total_cols = target_rows.shape[0]
    row_size = min(512, total_rows)
    row_count = total_rows // row_size
    col_size = min(1024, total_cols)

    def target_one_block(carried, operands):
        block, block_sq, block_pot = operands
        new_high = []
        new_sum = []
        for offset in range(0, total_cols, col_size):
            scores = (
                block_pot[:, None]
                - pair_cost(
                    block,
                    block_sq,
                    target_rows[offset : offset + col_size],
                    target_sq[offset : offset + col_size],
                )
            ) / EPS
            block_high = jnp.max(scores, axis=0)
            block_sum = jnp.sum(jnp.exp(scores - block_high[None, :]), axis=0)
            merged_high, merged_sum = combine_pairs(
                (carried[0][offset : offset + col_size], carried[1][offset : offset + col_size]),
                (block_high, block_sum),
            )
            new_high.append(merged_high)
            new_sum.append(merged_sum)
        return ((jnp.concatenate(new_high), jnp.concatenate(new_sum)), None)

    start_state = (
        jnp.full((total_cols,), -jnp.inf, jnp.float32),
        jnp.zeros((total_cols,), jnp.float32),
    )
    final_state, unused = lax.scan(
        target_one_block,
        start_state,
        (
            source_rows.reshape(row_count, row_size, source_rows.shape[1]),
            source_sq.reshape(row_count, row_size),
            source_pot.reshape(row_count, row_size),
        ),
    )
    return final_state


def careful(source, target):
    source_rows = lax.all_gather(source, "col", axis=0, tiled=True)
    target_rows = lax.all_gather(target, "row", axis=0, tiled=True)
    source_sq = jnp.sum(jnp.square(source_rows.astype(jnp.float32)), axis=1)
    target_sq = jnp.sum(jnp.square(target_rows.astype(jnp.float32)), axis=1)
    log_targets = jnp.log(jnp.float32(target_rows.shape[0] * lax.axis_size("col")))
    log_sources = jnp.log(jnp.float32(source_rows.shape[0] * lax.axis_size("row")))
    target_pot = jnp.zeros((target_rows.shape[0],), jnp.float32)
    source_pot = jnp.zeros((source_rows.shape[0],), jnp.float32)
    for sweep in range(ITERS):
        highest, summed = source_partials(
            source_rows, source_sq, target_rows, target_sq, target_pot
        )
        overall = lax.pmax(highest, "col")
        summed = lax.psum(summed * jnp.exp(highest - overall), "col")
        highest = overall
        source_pot = EPS * (log_targets - highest - jnp.log(summed))
        highest, summed = target_partials(
            source_rows, source_sq, target_rows, target_sq, source_pot
        )
        overall = lax.pmax(highest, "row")
        summed = lax.psum(summed * jnp.exp(highest - overall), "row")
        target_pot = EPS * (log_sources - overall - jnp.log(summed))
    return (source_pot, target_pot)


def log2(x):
    return jnp.log(x) * LOG2E


def split3(x):
    high = x.astype(BF16).astype(F32)
    mid = (x - high).astype(BF16).astype(F32)
    return high, mid, x - high - mid


def pick3(x, index, base, other):
    high, mid, low = split3(x)
    found = jnp.where(index == base + 1, mid, jnp.where(index == base + 2, low, other))
    return jnp.where(index == base, high, found).astype(BF16)


def nt_dot(x, y):
    return lax.dot_general(x, y, (((1,), (1,)), ((), ())), preferred_element_type=F32)


def kernel(
    row_n, col_n, s_ref, t_ref, f_ref, g_ref,
    s_all, t_all, s_ext, t_ext, kept, sums, highs, part, weight, s_sq, t_sq, shift_s, shift_t, from_col, from_row,
    s_send, s_recv, t_send, t_recv, pair_send, pair_recv, col_send, col_recv, row_send, row_recv,
):
    own_s, depth = s_ref.shape
    own_t = t_ref.shape[0]
    ns, nt = own_s * col_n, own_t * row_n
    total_s, total_t = float(ns * row_n), float(nt * col_n)
    my_row, my_col = lax.axis_index("row"), lax.axis_index("col")
    col_peers = [lax.rem(my_col + k, col_n) for k in range(1, col_n)]
    row_peers = [lax.rem(my_row + k, row_n) for k in range(1, row_n)]
    my_core = lax.rem(my_col, 2)
    twin = my_col + 1 - 2 * my_core
    chips = col_n // 2

    barrier = pltpu.get_barrier_semaphore()
    for peer in col_peers:
        pl.semaphore_signal(barrier, inc=1, device_id={"col": peer}, device_id_type=MESH)
    for peer in row_peers:
        pl.semaphore_signal(barrier, inc=1, device_id={"row": peer}, device_id_type=MESH)

    def s_block(index):
        return pl.ds(pl.multiple_of(index * own_s, own_s), own_s)

    def t_block(index):
        return pl.ds(pl.multiple_of(index * own_t, own_t), own_t)

    def s_from(k):
        return lax.rem(my_col - 2 * k + col_n, col_n)

    def twin_from(k):
        return lax.rem(twin - 2 * k + col_n, col_n)

    def t_from(k):
        return lax.rem(my_row - k + row_n, row_n)

    def t_copy(k):
        return pltpu.make_async_remote_copy(
            t_ref, t_all.at[t_block(my_row), :], t_send.at[k], t_recv.at[k],
            device_id={"row": lax.rem(my_row + k, row_n)}, device_id_type=MESH,
        )

    def s_copy(k):
        return pltpu.make_async_remote_copy(
            s_ref, s_all.at[s_block(my_col), :], s_send.at[k], s_recv.at[k],
            device_id={"col": lax.rem(my_col + 2 * k, col_n)}, device_id_type=MESH,
        )

    def twin_copy(k):
        at = s_all.at[s_block(s_from(k)), :]
        return pltpu.make_async_remote_copy(
            at, at, pair_send.at[k], pair_recv.at[k], device_id={"col": twin}, device_id_type=MESH
        )

    chunk = 128
    lane = lax.broadcasted_iota(jnp.int32, (chunk, depth), 1)
    first_ones = jnp.where(lane < 3, 1.0, 0.0)
    later_ones = jnp.where((lane >= 3) & (lane < 6), 1.0, 0.0)

    def spread(column):
        return jnp.broadcast_to(column, (chunk, depth))

    def t_prepare(block):
        def one(i, _):
            rows = pl.ds(pl.multiple_of(block * own_t + i * chunk, chunk), chunk)
            x = t_all[rows, :].astype(F32)
            square = x * x
            t_sq[:, rows] = jnp.sum(jnp.transpose(square), axis=0, keepdims=True)
            bias = spread(jnp.sum(square, axis=1, keepdims=True) * -0.5)
            t_ext[rows, :] = pick3(bias, lane, 0, later_ones)
            highs[rows, :] = jnp.full((chunk, depth), -3e38, F32)
            return 0

        lax.fori_loop(0, own_t // chunk, one, 0)

    def s_prepare(block):
        mine = t_block(my_row)
        sample = jnp.concatenate([t_ref[...], t_ext[mine, :]], axis=1)

        def one(i, _):
            rows = pl.ds(pl.multiple_of(block * own_s + i * chunk, chunk), chunk)
            x = s_all[rows, :]
            square = x.astype(F32) * x.astype(F32)
            s_sq[:, rows] = jnp.sum(jnp.transpose(square), axis=0, keepdims=True)
            seen = nt_dot(jnp.concatenate([x, first_ones.astype(BF16)], axis=1), sample)
            shift = spread(-FLOOR / SCALE - jnp.max(seen, axis=1, keepdims=True))
            shift_s[:, rows] = jnp.transpose(shift)[0:1, :]
            s_ext[rows, :] = pick3(shift, lane, 3, first_ones)
            return 0

        lax.fori_loop(0, own_s // chunk, one, 0)

    s_all[s_block(my_col), :] = s_ref[...]
    t_all[t_block(my_row), :] = t_ref[...]
    sums[...] = jnp.zeros_like(sums)
    t_prepare(my_row)
    s_prepare(my_col)

    pl.semaphore_wait(barrier, col_n + row_n - 2)
    for k in range(1, chips):
        s_copy(k).start()
    for k in range(1, row_n):
        t_copy(k).start()
    twin_copy(0).start()

    per = 2

    def terms_with(t_index, s_index):
        x = jnp.concatenate(
            [jnp.concatenate([t_all[t_block(i), :], t_ext[t_block(i), :]], axis=1) for i in t_index], axis=0
        )
        high = None
        for i in s_index:
            at = s_block(i)
            z = nt_dot(x, jnp.concatenate([s_all[at, :], s_ext[at, :]], axis=1))
            for c in range(0, own_s, depth):
                piece = z[:, c : c + depth]
                high = piece if high is None else jnp.maximum(high, piece)
            terms = jnp.exp2(z * SCALE).reshape(z.shape[0] // 8, 8, own_s)
            sums[:, at] = sums[:, at] + jnp.sum(terms, axis=0)
        for n, i in enumerate(t_index):
            at = t_block(i)
            highs[at, :] = jnp.maximum(highs[at, :], high[n * own_t : (n + 1) * own_t, :])

    for k in range(1, chips):
        s_copy(k).wait_recv()
        twin_copy(k).start()
        s_prepare(s_from(k))

    def near(p, _):
        @pl.when(p > 0)
        def _():
            t_copy(per * p).wait_recv()
            t_prepare(t_from(per * p))

        for j in range(1, per):
            t_copy(per * p + j).wait_recv()
            t_prepare(t_from(per * p + j))
        terms_with([t_from(per * p + j) for j in range(per)], [s_from(k) for k in range(chips)])
        return 0

    lax.fori_loop(0, row_n // per, near, 0)

    for k in range(chips):
        twin_copy(k).wait_recv()
        s_prepare(twin_from(k))

    def far(p, _):
        terms_with([t_from(per * p + j) for j in range(per)], [twin_from(k) for k in range(chips)])
        return 0

    lax.fori_loop(0, row_n // per, far, 0)

    for k in range(1, chips):
        s_copy(k).wait_send()
    for k in range(chips):
        twin_copy(k).wait_send()
    for k in range(1, row_n):
        t_copy(k).wait_send()

    def exchange(turn, sent, received, send, recv, axis, peers, meanwhile=None):
        copies = [
            pltpu.make_async_remote_copy(
                sent, received.at[turn, k], send.at[turn, k], recv.at[turn, k],
                device_id={axis: peer}, device_id_type=MESH,
            )
            for k, peer in enumerate(peers)
        ]
        for copy in copies:
            copy.start()
        if meanwhile is not None:
            meanwhile()
        for copy in copies:
            copy.wait()
        return [sent[...]] + [received[turn, k] for k in range(len(peers))]

    def over_col(turn, meanwhile=None):
        return exchange(turn, part.at[2 * turn], from_col, col_send, col_recv, "col", col_peers, meanwhile)

    def over_row(turn):
        return exchange(turn, part.at[2 * turn + 1], from_row, row_send, row_recv, "row", row_peers)

    def combined_logs(logs):
        highest = functools.reduce(jnp.maximum, logs)
        return highest + log2(sum(jnp.exp2(x - highest) for x in logs))

    def t_shift():
        room = (FLOOR + math.log2(total_t) - CEIL) / SCALE

        def one(i, _):
            rows = pl.ds(pl.multiple_of(i * chunk, chunk), chunk)
            bias = jnp.sum(jnp.where(lane < 3, t_ext[rows, :].astype(F32), 0.0), axis=1, keepdims=True)
            shift = spread(bias - jnp.max(highs[rows, :], axis=1, keepdims=True) - room)
            shift_t[:, rows] = jnp.transpose(shift)[0:1, :]
            t_ext[rows, :] = pick3(shift, lane, 3, first_ones)
            return 0

        lax.fori_loop(0, nt // chunk, one, 0)

    found = jnp.sum(sums[...], axis=0, keepdims=True)
    logs = log2(found) - shift_s[...] * SCALE
    part[0] = jnp.where(found < 2.0**120, logs, jnp.nan)
    f_first = math.log2(total_t) - combined_logs(over_col(0, t_shift))
    f_ref[...] = f_first

    def s_bias(i, _):
        rows = pl.ds(pl.multiple_of(i * chunk, chunk), chunk)
        bias = jnp.transpose(jnp.broadcast_to(f_ref[:, rows] * (1.0 / SCALE), (depth, chunk)))
        s_ext[rows, :] = pick3(bias, lane, 0, later_ones)
        return 0

    lax.fori_loop(0, ns // chunk, s_bias, 0)

    width = min(512, nt)
    step = min(2048, ns)

    def second(i, _):
        at = pl.ds(pl.multiple_of(i * width, width), width)
        w = jnp.concatenate([t_all[at, :], t_ext[at, :]], axis=1)
        summed = jnp.zeros((8, width), F32)
        for q in range(ns // step):
            rows = pl.ds(q * step, step)
            terms = jnp.exp2(nt_dot(jnp.concatenate([s_all[rows, :], s_ext[rows, :]], axis=1), w) * SCALE)
            kept[rows, at] = terms.astype(BF16)
            summed = summed + jnp.sum(terms.reshape(step // 8, 8, width), axis=0)
        part[1, :, at] = log2(jnp.sum(summed, axis=0, keepdims=True)) - shift_t[:, at] * SCALE
        return 0

    lax.fori_loop(0, nt // width, second, 0)
    logs = combined_logs(over_row(0))
    held = logs + shift_t[...] * SCALE
    g_first = jnp.where(held > -30.0, math.log2(total_s) - logs, jnp.nan)
    g_ref[...] = g_first
    weight[0] = jnp.exp2(g_first - shift_t[...] * SCALE)
    weight[1] = weight[0]

    def row_sums(out):
        fine = chunk // 2

        def one(i, _):
            pieces = []
            for h in range(0, chunk, fine):
                rows = pl.ds(pl.multiple_of(i * chunk, chunk) + h, fine)
                summed = jnp.zeros((fine, 128), F32)
                for c in range(0, nt, 128):
                    summed = summed + kept[rows, c : c + 128].astype(F32) * weight[1, :, c : c + 128]
                pieces.append(summed)
            turned = jnp.transpose(jnp.concatenate(pieces, axis=0))
            out[:, pl.ds(pl.multiple_of(i * chunk, chunk), chunk)] = jnp.sum(turned, axis=0, keepdims=True)
            return 0

        lax.fori_loop(0, ns // chunk, one, 0)

    def col_sums(x, out):
        wide = min(2048, nt)
        index = lax.broadcasted_iota(jnp.int32, (16, ns), 0)
        lhs = pick3(jnp.broadcast_to(x, (16, ns)), index, 0, 0.0)

        def one(i, _):
            at = pl.ds(pl.multiple_of(i * wide, wide), wide)
            got = jnp.dot(lhs, kept[:, at], preferred_element_type=F32)
            out[:, at] = jnp.sum(got, axis=0, keepdims=True) * weight[0, :, at]
            return 0

        lax.fori_loop(0, nt // wide, one, 0)

    for turn in range(1, ITERS):
        row_sums(part.at[2 * turn])
        u = total_t / sum(over_col(turn))
        col_sums(u, part.at[2 * turn + 1])
        v = total_s / sum(over_row(turn))
        weight[1] = weight[0] * v
    f_ref[...] = BACK * (f_ref[...] + log2(u)) + s_sq[...]
    g_ref[...] = BACK * (g_ref[...] + log2(v)) + t_sq[...]


def on_device(row_n, col_n, source, target):
    own_s, depth = source.shape
    own_t = target.shape[0]
    ns, nt = own_s * col_n, own_t * row_n
    vmem = pl.BlockSpec(memory_space=pltpu.VMEM)
    dma = pltpu.SemaphoreType.DMA
    f, g = pl.pallas_call(
        functools.partial(kernel, row_n, col_n),
        out_shape=(jax.ShapeDtypeStruct((1, ns), F32), jax.ShapeDtypeStruct((1, nt), F32)),
        in_specs=[vmem, vmem],
        out_specs=(vmem, vmem),
        scratch_shapes=[
            pltpu.VMEM((ns, depth), BF16),
            pltpu.VMEM((nt, depth), BF16),
            pltpu.VMEM((ns, depth), BF16),
            pltpu.VMEM((nt, depth), BF16),
            pltpu.VMEM((ns, nt), BF16),
            pltpu.VMEM((8, ns), F32),
            pltpu.VMEM((nt, depth), F32),
            pltpu.VMEM((2 * ITERS, 1, max(ns, nt)), F32),
            pltpu.VMEM((2, 1, nt), F32),
            pltpu.VMEM((1, ns), F32),
            pltpu.VMEM((1, nt), F32),
            pltpu.VMEM((1, ns), F32),
            pltpu.VMEM((1, nt), F32),
            pltpu.VMEM((ITERS, col_n - 1, 1, ns), F32),
            pltpu.VMEM((ITERS, row_n - 1, 1, nt), F32),
            dma((col_n // 2,)),
            dma((col_n // 2,)),
            dma((row_n,)),
            dma((row_n,)),
            dma((col_n // 2,)),
            dma((col_n // 2,)),
            dma((ITERS, col_n - 1)),
            dma((ITERS, col_n - 1)),
            dma((ITERS, row_n - 1)),
            dma((ITERS, row_n - 1)),
        ],
        compiler_params=pltpu.CompilerParams(
            collective_id=0, has_side_effects=True, vmem_limit_bytes=60 << 20
        ),
        cost_estimate=pl.CostEstimate(
            flops=12 * ns * nt * depth, bytes_accessed=2 * (ns + nt) * depth, transcendentals=2 * ns * nt
        ),
    )(source, target)
    fast = f.reshape(ns), g.reshape(nt)
    return lax.cond(jnp.isnan(fast[0][0]), lambda: careful(source, target), lambda: fast)


def solution(mesh):
    placed = (P(("row", "col"), None), P(("col", "row"), None))
    return jax.shard_map(
        functools.partial(on_device, mesh.shape["row"], mesh.shape["col"]),
        mesh=mesh,
        in_specs=placed,
        out_specs=(P("row"), P("col")),
        check_vma=False,
    )
```

```python
import functools
import math

import jax
import jax.numpy as jnp
from jax import lax
from jax.experimental import pallas as pl
from jax.experimental.pallas import tpu as pltpu
from jax.sharding import PartitionSpec as P

ITERS = 3
EPS = 0.02
LOG2E = 1.0 / math.log(2.0)
SCALE = 2.0 * LOG2E / EPS
BACK = EPS / LOG2E
FLOOR = 90.0
CEIL = 100.0
F32 = jnp.float32
BF16 = jnp.bfloat16
MESH = pl.DeviceIdType.MESH


def log2(x):
    return jnp.log(x) * LOG2E


def split3(x):
    high = x.astype(BF16).astype(F32)
    mid = (x - high).astype(BF16).astype(F32)
    return high, mid, x - high - mid


def pick3(x, index, base, other):
    high, mid, low = split3(x)
    found = jnp.where(index == base + 1, mid, jnp.where(index == base + 2, low, other))
    return jnp.where(index == base, high, found).astype(BF16)


def nt_dot(x, y):
    return lax.dot_general(x, y, (((1,), (1,)), ((), ())), preferred_element_type=F32)


def kernel(
    row_n, col_n, s_ref, t_ref, f_ref, g_ref,
    s_all, t_all, s_ext, t_ext, kept, sums, highs, part, weight, s_sq, t_sq, shift_s, shift_t, from_col, from_row,
    s_send, s_recv, t_send, t_recv, pair_send, pair_recv, col_send, col_recv, row_send, row_recv,
):
    own_s, depth = s_ref.shape
    own_t = t_ref.shape[0]
    ns, nt = own_s * col_n, own_t * row_n
    total_s, total_t = float(ns * row_n), float(nt * col_n)
    my_row, my_col = lax.axis_index("row"), lax.axis_index("col")
    col_peers = [lax.rem(my_col + k, col_n) for k in range(1, col_n)]
    row_peers = [lax.rem(my_row + k, row_n) for k in range(1, row_n)]
    my_core = lax.rem(my_col, 2)
    twin = my_col + 1 - 2 * my_core
    chips = col_n // 2

    barrier = pltpu.get_barrier_semaphore()
    for peer in col_peers:
        pl.semaphore_signal(barrier, inc=1, device_id={"col": peer}, device_id_type=MESH)
    for peer in row_peers:
        pl.semaphore_signal(barrier, inc=1, device_id={"row": peer}, device_id_type=MESH)

    def s_block(index):
        return pl.ds(pl.multiple_of(index * own_s, own_s), own_s)

    def t_block(index):
        return pl.ds(pl.multiple_of(index * own_t, own_t), own_t)

    def s_from(k):
        return lax.rem(my_col - 2 * k + col_n, col_n)

    def twin_from(k):
        return lax.rem(twin - 2 * k + col_n, col_n)

    def t_from(k):
        return lax.rem(my_row - k + row_n, row_n)

    def t_copy(k):
        return pltpu.make_async_remote_copy(
            t_ref, t_all.at[t_block(my_row), :], t_send.at[k], t_recv.at[k],
            device_id={"row": lax.rem(my_row + k, row_n)}, device_id_type=MESH,
        )

    def s_copy(k):
        return pltpu.make_async_remote_copy(
            s_ref, s_all.at[s_block(my_col), :], s_send.at[k], s_recv.at[k],
            device_id={"col": lax.rem(my_col + 2 * k, col_n)}, device_id_type=MESH,
        )

    def twin_copy(k):
        at = s_all.at[s_block(s_from(k)), :]
        return pltpu.make_async_remote_copy(
            s_ref if k == 0 else at, at, pair_send.at[k], pair_recv.at[k], device_id={"col": twin}, device_id_type=MESH
        )

    pl.semaphore_wait(barrier, col_n + row_n - 2)
    for k in range(1, chips):
        s_copy(k).start()
    twin_copy(0).start()
    for k in range(1, row_n):
        t_copy(k).start()

    chunk = 128

    def ones_at(rows, first):
        lane = lax.broadcasted_iota(jnp.int32, (rows, depth), 1)
        return lane, jnp.where((lane >= first) & (lane < first + 3), 1.0, 0.0)

    def spread(column):
        return jnp.broadcast_to(column, (column.shape[0], depth))

    def along_lanes(ext, first):
        select = ones_at(16, first)[1].astype(BF16)
        return nt_dot(select, ext[...])[0:1, :]

    def t_prepare(index):
        lane, ones = ones_at(own_t, 3)
        for i in index:
            x = t_all[t_block(i), :].astype(F32)
            bias = spread(jnp.sum(x * x, axis=1, keepdims=True) * -0.5)
            t_ext[t_block(i), :] = pick3(bias, lane, 0, ones)

    def s_prepare(i):
        lane, ones = ones_at(own_s, 0)
        sample = jnp.concatenate([t_ref[...], t_ext[t_block(my_row), :]], axis=1)
        x = jnp.concatenate([s_all[s_block(i), :], ones.astype(BF16)], axis=1)
        shift = spread(-FLOOR / SCALE - jnp.max(nt_dot(x, sample), axis=1, keepdims=True))
        s_ext[s_block(i), :] = pick3(shift, lane, 3, ones)

    s_all[s_block(my_col), :] = s_ref[...]
    t_all[t_block(my_row), :] = t_ref[...]
    sums[...] = jnp.zeros_like(sums)
    t_prepare([my_row])
    s_prepare(my_col)

    per = 2

    def terms_with(t_index, s_index):
        x = jnp.concatenate(
            [jnp.concatenate([t_all[t_block(i), :], t_ext[t_block(i), :]], axis=1) for i in t_index], axis=0
        )
        high = None
        for i in s_index:
            at = s_block(i)
            z = nt_dot(x, jnp.concatenate([s_all[at, :], s_ext[at, :]], axis=1))
            for c in range(0, own_s, depth):
                piece = z[:, c : c + depth]
                high = piece if high is None else jnp.maximum(high, piece)
            terms = jnp.exp2(z * SCALE).reshape(z.shape[0] // 8, 8, own_s)
            sums[:, at] = sums[:, at] + jnp.sum(terms, axis=0)
        for n, i in enumerate(t_index):
            at = t_block(i)
            highs[at, :] = jnp.maximum(highs[at, :], high[n * own_t : (n + 1) * own_t, :])

    for k in range(1, chips):
        s_copy(k).wait_recv()
        twin_copy(k).start()
        s_prepare(s_from(k))

    for j in range(1, per):
        t_copy(j).wait_recv()
    t_prepare([t_from(j) for j in range(1, per)])
    highs[...] = jnp.full_like(highs, -3e38)

    def near(p, _):
        terms_with([t_from(per * p + j) for j in range(per)], [s_from(k) for k in range(chips)])

        @pl.when(p < row_n // per - 1)
        def _():
            following = [per * p + per + j for j in range(per)]
            for k in following:
                t_copy(k).wait_recv()
            t_prepare([t_from(k) for k in following])

        return 0

    lax.fori_loop(0, row_n // per, near, 0)

    for k in range(chips):
        twin_copy(k).wait_recv()
        s_prepare(twin_from(k))

    def far(p, _):
        terms_with([t_from(per * p + j) for j in range(per)], [twin_from(k) for k in range(chips)])
        return 0

    lax.fori_loop(0, row_n // per, far, 0)

    for k in range(1, chips):
        s_copy(k).wait_send()
    for k in range(chips):
        twin_copy(k).wait_send()
    for k in range(1, row_n):
        t_copy(k).wait_send()

    def exchange(turn, sent, received, send, recv, axis, peers, meanwhile=None):
        copies = [
            pltpu.make_async_remote_copy(
                sent, received.at[turn, k], send.at[turn, k], recv.at[turn, k],
                device_id={axis: peer}, device_id_type=MESH,
            )
            for k, peer in enumerate(peers)
        ]
        for copy in copies:
            copy.start()
        if meanwhile is not None:
            meanwhile()
        for copy in copies:
            copy.wait()
        return [sent[...]] + [received[turn, k] for k in range(len(peers))]

    def over_col(turn, meanwhile=None):
        return exchange(turn, part.at[2 * turn], from_col, col_send, col_recv, "col", col_peers, meanwhile)

    def over_row(turn, meanwhile=None):
        return exchange(turn, part.at[2 * turn + 1], from_row, row_send, row_recv, "row", row_peers, meanwhile)

    def s_norms():
        ones = jnp.full((16, depth), 1.0, BF16)

        def one(i, _):
            rows = pl.ds(pl.multiple_of(i * own_s, own_s), own_s)
            x = s_all[rows, :].astype(F32)
            square = x * x
            high = square.astype(BF16)
            low = (square - high.astype(F32)).astype(BF16)
            s_sq[:, rows] = (nt_dot(ones, high) + nt_dot(ones, low))[0:1, :]
            return 0

        lax.fori_loop(0, col_n, one, 0)

    def combined_logs(logs):
        highest = functools.reduce(jnp.maximum, logs)
        return highest + log2(sum(jnp.exp2(x - highest) for x in logs))

    def t_shift():
        room = (FLOOR + math.log2(total_t) - CEIL) / SCALE

        t_sq[...] = -2.0 * along_lanes(t_ext, 0)
        size = min(512, nt)
        lane, ones = ones_at(size, 0)

        def one(i, _):
            rows = pl.ds(pl.multiple_of(i * size, size), size)
            bias = jnp.sum(jnp.where(lane < 3, t_ext[rows, :].astype(F32), 0.0), axis=1, keepdims=True)
            shift = spread(bias - jnp.max(highs[rows, :], axis=1, keepdims=True) - room)
            t_ext[rows, :] = pick3(shift, lane, 3, ones)
            return 0

        lax.fori_loop(0, nt // size, one, 0)
        shift_t[...] = along_lanes(t_ext, 3)

    shift_s[...] = along_lanes(s_ext, 3)
    found = jnp.sum(sums[...], axis=0, keepdims=True)
    logs = log2(found) - shift_s[...] * SCALE
    part[0] = jnp.where(found < 2.0**120, logs, jnp.nan)
    f_first = math.log2(total_t) - combined_logs(over_col(0, t_shift))
    f_ref[...] = f_first

    def s_bias(i, _):
        size = min(512, ns)
        lane, ones = ones_at(size, 3)
        rows = pl.ds(pl.multiple_of(i * size, size), size)
        bias = jnp.transpose(jnp.broadcast_to(f_ref[:, rows] * (1.0 / SCALE), (depth, size)))
        s_ext[rows, :] = pick3(bias, lane, 0, ones)
        return 0

    lax.fori_loop(0, ns // min(512, ns), s_bias, 0)

    width = min(512, nt)
    step = min(2048, ns)

    def second(i, _):
        at = pl.ds(pl.multiple_of(i * width, width), width)
        w = jnp.concatenate([t_all[at, :], t_ext[at, :]], axis=1)
        summed = jnp.zeros((8, width), F32)
        for q in range(ns // step):
            rows = pl.ds(q * step, step)
            terms = jnp.exp2(nt_dot(jnp.concatenate([s_all[rows, :], s_ext[rows, :]], axis=1), w) * SCALE)
            kept[rows, at] = terms.astype(BF16)
            summed = summed + jnp.sum(terms.reshape(step // 8, 8, width), axis=0)
        part[1, :, at] = log2(jnp.sum(summed, axis=0, keepdims=True)) - shift_t[:, at] * SCALE
        return 0

    lax.fori_loop(0, nt // width, second, 0)
    logs = combined_logs(over_row(0, s_norms))
    held = logs + shift_t[...] * SCALE
    g_first = jnp.where(held > -30.0, math.log2(total_s) - logs, jnp.nan)
    g_ref[...] = g_first
    weight[0] = jnp.exp2(g_first - shift_t[...] * SCALE)
    weight[1] = weight[0]

    def row_sums(out):
        fine = chunk // 2

        def one(i, _):
            pieces = []
            for h in range(0, chunk, fine):
                rows = pl.ds(pl.multiple_of(i * chunk, chunk) + h, fine)
                summed = jnp.zeros((fine, 128), F32)
                for c in range(0, nt, 128):
                    summed = summed + kept[rows, c : c + 128].astype(F32) * weight[1, :, c : c + 128]
                pieces.append(summed)
            turned = jnp.transpose(jnp.concatenate(pieces, axis=0))
            out[:, pl.ds(pl.multiple_of(i * chunk, chunk), chunk)] = jnp.sum(turned, axis=0, keepdims=True)
            return 0

        lax.fori_loop(0, ns // chunk, one, 0)

    def col_sums(x, out):
        wide = min(2048, nt)
        index = lax.broadcasted_iota(jnp.int32, (16, ns), 0)
        lhs = pick3(jnp.broadcast_to(x, (16, ns)), index, 0, 0.0)

        def one(i, _):
            at = pl.ds(pl.multiple_of(i * wide, wide), wide)
            got = jnp.dot(lhs, kept[:, at], preferred_element_type=F32)
            out[:, at] = jnp.sum(got, axis=0, keepdims=True) * weight[0, :, at]
            return 0

        lax.fori_loop(0, nt // wide, one, 0)

    for turn in range(1, ITERS):
        row_sums(part.at[2 * turn])
        u = total_t / sum(over_col(turn))
        col_sums(u, part.at[2 * turn + 1])
        v = total_s / sum(over_row(turn))
        weight[1] = weight[0] * v
    f_ref[...] = BACK * (f_ref[...] + log2(u)) + s_sq[...]
    g_ref[...] = BACK * (g_ref[...] + log2(v)) + t_sq[...]


def careful_kernel(
    row_n, col_n, s_ref, t_ref, f_ref, g_ref,
    s_all, t_all, s_ext, t_ext, kept, z0, z1, part, col_high, s_sq, t_sq, from_col, from_row,
    s_send, s_recv, t_send, t_recv, col_send, col_recv, row_send, row_recv,
):
    own_s, depth = s_ref.shape
    own_t = t_ref.shape[0]
    ns, nt = own_s * col_n, own_t * row_n
    total_s, total_t = float(ns * row_n), float(nt * col_n)
    my_row, my_col = lax.axis_index("row"), lax.axis_index("col")
    col_peers = [lax.rem(my_col + k, col_n) for k in range(1, col_n)]
    row_peers = [lax.rem(my_row + k, row_n) for k in range(1, row_n)]

    barrier = pltpu.get_barrier_semaphore()
    for peer in col_peers:
        pl.semaphore_signal(barrier, inc=1, device_id={"col": peer}, device_id_type=MESH)
    for peer in row_peers:
        pl.semaphore_signal(barrier, inc=1, device_id={"row": peer}, device_id_type=MESH)
    pl.semaphore_wait(barrier, col_n + row_n - 2)

    s_rows = pl.ds(pl.multiple_of(my_col * own_s, own_s), own_s)
    t_rows = pl.ds(pl.multiple_of(my_row * own_t, own_t), own_t)
    gathers = []
    for k, peer in enumerate(row_peers):
        gathers.append(
            pltpu.make_async_remote_copy(
                t_ref, t_all.at[t_rows, :], t_send.at[k], t_recv.at[k],
                device_id={"row": peer}, device_id_type=MESH,
            )
        )
    for k, peer in enumerate(col_peers):
        gathers.append(
            pltpu.make_async_remote_copy(
                s_ref, s_all.at[s_rows, :], s_send.at[k], s_recv.at[k],
                device_id={"col": peer}, device_id_type=MESH,
            )
        )
    for copy in gathers:
        copy.start()
    s_all[s_rows, :] = s_ref[...]
    t_all[t_rows, :] = t_ref[...]
    for copy in gathers:
        copy.wait()

    chunk = min(512, own_s, own_t)
    lane = lax.broadcasted_iota(jnp.int32, (chunk, depth), 1)
    ones = jnp.where(lane < 3, 1.0, 0.0).astype(BF16)

    def s_prepare(i, _):
        rows = pl.ds(pl.multiple_of(i * chunk, chunk), chunk)
        x = s_all[rows, :].astype(F32)
        s_sq[:, rows] = jnp.sum(jnp.transpose(x * x), axis=0, keepdims=True)
        s_ext[rows, :] = ones
        return 0

    def t_prepare(i, _):
        rows = pl.ds(pl.multiple_of(i * chunk, chunk), chunk)
        x = t_all[rows, :].astype(F32)
        t_sq[:, rows] = jnp.sum(jnp.transpose(x * x), axis=0, keepdims=True)
        bias = jnp.sum(x * x, axis=1, keepdims=True) * -0.5
        t_ext[rows, :] = pick3(jnp.broadcast_to(bias, (chunk, depth)), lane, 0, 0.0)
        return 0

    lax.fori_loop(0, ns // chunk, s_prepare, 0)
    lax.fori_loop(0, nt // chunk, t_prepare, 0)

    def logs_pass(x_all, x_ext, w_all, w_ext, out, keep):
        nx, nw = x_all.shape[0], w_all.shape[0]
        width = z0.shape[1]
        tiles = nw // width
        step = min(512, nx)
        fine = min(64, step)

        def lanes(tile):
            return pl.ds(pl.multiple_of(tile * width, width), width)

        def scores(tile, q, z, highest):
            rows = pl.ds(q * step, step)
            at = lanes(tile)
            x = jnp.concatenate([x_all[rows, :], x_ext[rows, :]], axis=1)
            w = jnp.concatenate([w_all[at, :], w_ext[at, :]], axis=1)
            inner = nt_dot(x, w)
            z[rows, :] = inner
            return jnp.maximum(highest, jnp.max(inner.reshape(step // 8, 8, width), axis=0))

        def sums(tile, q, z, highest, summed):
            for j in range(q * step, (q + 1) * step, fine):
                rows = pl.ds(j, fine)
                shifted = z[rows, :].reshape(fine // 8, 8, width) - highest[None]
                terms = jnp.exp2(shifted * SCALE)
                if keep:
                    kept[rows, lanes(tile)] = terms.reshape(fine, width).astype(BF16)
                summed = summed + jnp.sum(terms, axis=0)
            return summed

        def settle(highest):
            return jnp.broadcast_to(jnp.max(highest, axis=0, keepdims=True), (8, width))

        low = jnp.full((8, width), -3e38, F32)

        def both(tile, z_now, highest, z_next):
            following = jnp.minimum(tile + 1, tiles - 1)
            new_high = low
            summed = jnp.zeros((8, width), F32)
            for q in range(nx // step):
                new_high = scores(following, q, z_next, new_high)
                summed = sums(tile, q, z_now, highest, summed)
            top = highest[0:1, :] * SCALE
            out[:, lanes(tile)] = top + log2(jnp.sum(summed, axis=0, keepdims=True))
            if keep:
                col_high[:, lanes(tile)] = top
            return settle(new_high)

        def pair(i, highest):
            highest = both(2 * i, z0, highest, z1)
            return both(2 * i + 1, z1, highest, z0)

        first = low
        for q in range(nx // step):
            first = scores(0, q, z0, first)
        lax.fori_loop(0, tiles // 2, pair, settle(first))

    def exchange(turn, sent, received, send, recv, axis, peers):
        copies = [
            pltpu.make_async_remote_copy(
                sent, received.at[turn, k], send.at[turn, k], recv.at[turn, k],
                device_id={axis: peer}, device_id_type=MESH,
            )
            for k, peer in enumerate(peers)
        ]
        for copy in copies:
            copy.start()
        for copy in copies:
            copy.wait()
        return [sent[...]] + [received[turn, k] for k in range(len(peers))]

    def over_col(turn):
        return exchange(turn, part.at[2 * turn], from_col, col_send, col_recv, "col", col_peers)

    def over_row(turn):
        return exchange(turn, part.at[2 * turn + 1], from_row, row_send, row_recv, "row", row_peers)

    def combined_logs(logs):
        highest = functools.reduce(jnp.maximum, logs)
        return highest + log2(sum(jnp.exp2(x - highest) for x in logs))

    logs_pass(t_all, t_ext, s_all, s_ext, part.at[0], False)
    f_first = math.log2(total_t) - combined_logs(over_col(0))
    f_ref[...] = f_first

    def s_bias(i, _):
        rows = pl.ds(pl.multiple_of(i * chunk, chunk), chunk)
        bias = jnp.transpose(jnp.broadcast_to(f_ref[:, rows] * (1.0 / SCALE), (depth, chunk)))
        s_ext[rows, :] = pick3(bias, lane, 0, 0.0)
        return 0

    def t_ones(i, _):
        t_ext[pl.ds(pl.multiple_of(i * chunk, chunk), chunk), :] = ones
        return 0

    lax.fori_loop(0, ns // chunk, s_bias, 0)
    lax.fori_loop(0, nt // chunk, t_ones, 0)
    logs_pass(s_all, s_ext, t_all, t_ext, part.at[1], True)
    g_first = math.log2(total_s) - combined_logs(over_row(0))
    g_ref[...] = g_first
    col_high[...] = jnp.exp2(g_first + col_high[...])

    block = min(512, ns, nt)

    def parts_of(x):
        index = lax.broadcasted_iota(jnp.int32, (16, x.shape[1]), 0)
        return pick3(jnp.broadcast_to(x, (16, x.shape[1])), index, 0, 0.0)

    def row_sums(x, out):
        lhs = parts_of(x)

        def one(i, _):
            rows = pl.ds(pl.multiple_of(i * block, block), block)
            out[:, rows] = jnp.sum(nt_dot(lhs, kept[rows, :]), axis=0, keepdims=True)
            return 0

        lax.fori_loop(0, ns // block, one, 0)

    def col_sums(x, out):
        lhs = parts_of(x)

        def one(i, _):
            at = pl.ds(pl.multiple_of(i * block, block), block)
            found = jnp.dot(lhs, kept[:, at], preferred_element_type=F32)
            out[:, at] = jnp.sum(found, axis=0, keepdims=True) * col_high[:, at]
            return 0

        lax.fori_loop(0, nt // block, one, 0)

    weight = col_high[...]
    for turn in range(1, ITERS):
        row_sums(weight, part.at[2 * turn])
        u = total_t / sum(over_col(turn))
        col_sums(u, part.at[2 * turn + 1])
        v = total_s / sum(over_row(turn))
        weight = col_high[...] * v
    f_ref[...] = BACK * (f_ref[...] + log2(u)) + s_sq[...]
    g_ref[...] = BACK * (g_ref[...] + log2(v)) + t_sq[...]


def careful(row_n, col_n, source, target):
    own_s, depth = source.shape
    own_t = target.shape[0]
    ns, nt = own_s * col_n, own_t * row_n
    width = min(256, ns // 2, nt // 2)
    vmem = pl.BlockSpec(memory_space=pltpu.VMEM)
    dma = pltpu.SemaphoreType.DMA
    f, g = pl.pallas_call(
        functools.partial(careful_kernel, row_n, col_n),
        out_shape=(jax.ShapeDtypeStruct((1, ns), F32), jax.ShapeDtypeStruct((1, nt), F32)),
        in_specs=[vmem, vmem],
        out_specs=(vmem, vmem),
        scratch_shapes=[
            pltpu.VMEM((ns, depth), BF16),
            pltpu.VMEM((nt, depth), BF16),
            pltpu.VMEM((ns, depth), BF16),
            pltpu.VMEM((nt, depth), BF16),
            pltpu.VMEM((ns, nt), BF16),
            pltpu.VMEM((max(ns, nt), width), F32),
            pltpu.VMEM((max(ns, nt), width), F32),
            pltpu.VMEM((2 * ITERS, 1, max(ns, nt)), F32),
            pltpu.VMEM((1, nt), F32),
            pltpu.VMEM((1, ns), F32),
            pltpu.VMEM((1, nt), F32),
            pltpu.VMEM((ITERS, col_n - 1, 1, ns), F32),
            pltpu.VMEM((ITERS, row_n - 1, 1, nt), F32),
            dma((col_n - 1,)),
            dma((col_n - 1,)),
            dma((row_n - 1,)),
            dma((row_n - 1,)),
            dma((ITERS, col_n - 1)),
            dma((ITERS, col_n - 1)),
            dma((ITERS, row_n - 1)),
            dma((ITERS, row_n - 1)),
        ],
        compiler_params=pltpu.CompilerParams(
            collective_id=1, has_side_effects=True, vmem_limit_bytes=60 << 20
        ),
        cost_estimate=pl.CostEstimate(
            flops=12 * ns * nt * depth, bytes_accessed=2 * (ns + nt) * depth, transcendentals=2 * ns * nt
        ),
    )(source, target)
    return f.reshape(ns), g.reshape(nt)


def on_device(row_n, col_n, source, target):
    own_s, depth = source.shape
    own_t = target.shape[0]
    ns, nt = own_s * col_n, own_t * row_n
    vmem = pl.BlockSpec(memory_space=pltpu.VMEM)
    dma = pltpu.SemaphoreType.DMA
    f, g = pl.pallas_call(
        functools.partial(kernel, row_n, col_n),
        out_shape=(jax.ShapeDtypeStruct((1, ns), F32), jax.ShapeDtypeStruct((1, nt), F32)),
        in_specs=[vmem, vmem],
        out_specs=(vmem, vmem),
        scratch_shapes=[
            pltpu.VMEM((ns, depth), BF16),
            pltpu.VMEM((nt, depth), BF16),
            pltpu.VMEM((ns, depth), BF16),
            pltpu.VMEM((nt, depth), BF16),
            pltpu.VMEM((ns, nt), BF16),
            pltpu.VMEM((8, ns), F32),
            pltpu.VMEM((nt, depth), F32),
            pltpu.VMEM((2 * ITERS, 1, max(ns, nt)), F32),
            pltpu.VMEM((2, 1, nt), F32),
            pltpu.VMEM((1, ns), F32),
            pltpu.VMEM((1, nt), F32),
            pltpu.VMEM((1, ns), F32),
            pltpu.VMEM((1, nt), F32),
            pltpu.VMEM((ITERS, col_n - 1, 1, ns), F32),
            pltpu.VMEM((ITERS, row_n - 1, 1, nt), F32),
            dma((col_n // 2,)),
            dma((col_n // 2,)),
            dma((row_n,)),
            dma((row_n,)),
            dma((col_n // 2,)),
            dma((col_n // 2,)),
            dma((ITERS, col_n - 1)),
            dma((ITERS, col_n - 1)),
            dma((ITERS, row_n - 1)),
            dma((ITERS, row_n - 1)),
        ],
        compiler_params=pltpu.CompilerParams(
            collective_id=0, has_side_effects=True, vmem_limit_bytes=60 << 20
        ),
        cost_estimate=pl.CostEstimate(
            flops=12 * ns * nt * depth, bytes_accessed=2 * (ns + nt) * depth, transcendentals=2 * ns * nt
        ),
    )(source, target)
    fast = f.reshape(ns), g.reshape(nt)
    return lax.cond(jnp.isnan(f[0, 0]), lambda: careful(row_n, col_n, source, target), lambda: fast)


def solution(mesh):
    placed = (P(("row", "col"), None), P(("col", "row"), None))
    return jax.shard_map(
        functools.partial(on_device, mesh.shape["row"], mesh.shape["col"]),
        mesh=mesh,
        in_specs=placed,
        out_specs=(P("row"), P("col")),
        check_vma=False,
    )
```

```python
import functools
import math

import jax
import jax.numpy as jnp
from jax import lax
from jax.experimental import pallas as pl
from jax.experimental.pallas import tpu as pltpu
from jax.sharding import PartitionSpec as P

ITERS = 3
EPS = 0.02
LOG2E = 1.0 / math.log(2.0)
SCALE = 2.0 * LOG2E / EPS
BACK = EPS / LOG2E
FLOOR = 90.0
CEIL = 100.0
F32 = jnp.float32
BF16 = jnp.bfloat16
MESH = pl.DeviceIdType.MESH


def log2(x):
    return jnp.log(x) * LOG2E


def split3(x):
    high = x.astype(BF16).astype(F32)
    mid = (x - high).astype(BF16).astype(F32)
    return high, mid, x - high - mid


def pick3(x, index, base, other):
    high, mid, low = split3(x)
    found = jnp.where(index == base + 1, mid, jnp.where(index == base + 2, low, other))
    return jnp.where(index == base, high, found).astype(BF16)


def nt_dot(x, y):
    return lax.dot_general(x, y, (((1,), (1,)), ((), ())), preferred_element_type=F32)


def kernel(
    row_n, col_n, s_ref, t_ref, f_ref, g_ref,
    s_all, t_all, s_ext, t_ext, kept, sums, sums_t, highs, row_part, col_part, part, weight, s_sq, t_sq, shift_s, shift_t,
    from_col, from_row,
    s_send, s_recv, t_send, t_recv, pair_send, pair_recv, col_send, col_recv, row_send, row_recv,
):
    own_s, depth = s_ref.shape
    own_t = t_ref.shape[0]
    ns, nt = own_s * col_n, own_t * row_n
    total_s, total_t = float(ns * row_n), float(nt * col_n)
    my_row, my_col = lax.axis_index("row"), lax.axis_index("col")
    col_peers = [lax.rem(my_col + k, col_n) for k in range(1, col_n)]
    row_peers = [lax.rem(my_row + k, row_n) for k in range(1, row_n)]
    my_core = lax.rem(my_col, 2)
    twin = my_col + 1 - 2 * my_core
    chips = col_n // 2

    barrier = pltpu.get_barrier_semaphore()
    for peer in col_peers:
        pl.semaphore_signal(barrier, inc=1, device_id={"col": peer}, device_id_type=MESH)
    for peer in row_peers:
        pl.semaphore_signal(barrier, inc=1, device_id={"row": peer}, device_id_type=MESH)

    def s_block(index):
        return pl.ds(pl.multiple_of(index * own_s, own_s), own_s)

    def t_block(index):
        return pl.ds(pl.multiple_of(index * own_t, own_t), own_t)

    def s_from(k):
        return lax.rem(my_col - 2 * k + col_n, col_n)

    def twin_from(k):
        return lax.rem(twin - 2 * k + col_n, col_n)

    def t_from(k):
        return lax.rem(my_row - k + row_n, row_n)

    def t_copy(k):
        return pltpu.make_async_remote_copy(
            t_ref, t_all.at[t_block(my_row), :], t_send.at[k], t_recv.at[k],
            device_id={"row": lax.rem(my_row + k, row_n)}, device_id_type=MESH,
        )

    def s_copy(k):
        return pltpu.make_async_remote_copy(
            s_ref, s_all.at[s_block(my_col), :], s_send.at[k], s_recv.at[k],
            device_id={"col": lax.rem(my_col + 2 * k, col_n)}, device_id_type=MESH,
        )

    def twin_copy(k):
        at = s_all.at[s_block(s_from(k)), :]
        return pltpu.make_async_remote_copy(
            s_ref if k == 0 else at, at, pair_send.at[k], pair_recv.at[k], device_id={"col": twin}, device_id_type=MESH
        )

    pl.semaphore_wait(barrier, col_n + row_n - 2)
    for k in range(1, chips):
        s_copy(k).start()
    twin_copy(0).start()
    for k in range(1, row_n):
        t_copy(k).start()

    chunk = 128

    def ones_at(rows, first):
        lane = lax.broadcasted_iota(jnp.int32, (rows, depth), 1)
        return lane, jnp.where((lane >= first) & (lane < first + 3), 1.0, 0.0)

    def spread(column):
        return jnp.broadcast_to(column, (column.shape[0], depth))

    def along_lanes(ext, first):
        select = ones_at(16, first)[1].astype(BF16)
        return nt_dot(select, ext)[0:1, :]

    def t_prepare(index):
        lane, ones = ones_at(own_t, 3)
        for i in index:
            x = t_all[t_block(i), :].astype(F32)
            bias = spread(jnp.sum(x * x, axis=1, keepdims=True) * -0.5)
            t_ext[t_block(i), :] = pick3(bias, lane, 0, ones)

    def s_prepare(i):
        lane, ones = ones_at(own_s, 0)
        sample = jnp.concatenate([t_ref[...], t_ext[t_block(my_row), :]], axis=1)
        x = jnp.concatenate([s_all[s_block(i), :], ones.astype(BF16)], axis=1)
        shift = spread(-FLOOR / SCALE - jnp.max(nt_dot(x, sample), axis=1, keepdims=True))
        s_ext[s_block(i), :] = pick3(shift, lane, 3, ones)

    s_all[s_block(my_col), :] = s_ref[...]
    t_all[t_block(my_row), :] = t_ref[...]
    sums[...] = jnp.zeros_like(sums)
    t_prepare([my_row])
    s_prepare(my_col)

    per = 2
    half_s, half_t = ns // 2, nt // 2
    halves = (0, 1)

    def s_half(h):
        return pl.ds(h * half_s, half_s)

    def t_half(h):
        return pl.ds(h * half_t, half_t)

    def terms_with(t_index, h):
        x = jnp.concatenate(
            [jnp.concatenate([t_all[t_block(i), :], t_ext[t_block(i), :]], axis=1) for i in t_index], axis=0
        )
        high = None
        for i in range(h * col_n // 2, (h + 1) * col_n // 2):
            at = pl.ds(i * own_s, own_s)
            z = nt_dot(x, jnp.concatenate([s_all[at, :], s_ext[at, :]], axis=1))
            for c in range(0, own_s, depth):
                piece = z[:, c : c + depth]
                high = piece if high is None else jnp.maximum(high, piece)
            terms = jnp.exp2(z * SCALE).reshape(z.shape[0] // 8, 8, own_s)
            sums[:, at] = sums[:, at] + jnp.sum(terms, axis=0)
        for n, i in enumerate(t_index):
            at = t_block(i)
            highs[at, :] = jnp.maximum(highs[at, :], high[n * own_t : (n + 1) * own_t, :])

    def over(axis, turn, h):
        if axis == "col":
            here, there, send, recv, peers, at = part.at[2 * turn], from_col, col_send, col_recv, col_peers, s_half(h)
        else:
            here, there, send, recv, peers, at = part.at[2 * turn + 1], from_row, row_send, row_recv, row_peers, t_half(h)
        return [
            pltpu.make_async_remote_copy(
                here.at[:, at], there.at[turn, k, :, at], send.at[turn, h, k], recv.at[turn, h, k],
                device_id={axis: peer}, device_id_type=MESH,
            )
            for k, peer in enumerate(peers)
        ]

    def start(axis, turn, h):
        for copy in over(axis, turn, h):
            copy.start()

    def finish(axis, turn, h):
        for copy in over(axis, turn, h):
            copy.wait()
        if axis == "col":
            return [part[2 * turn, :, s_half(h)]] + [from_col[turn, k, :, s_half(h)] for k in range(col_n - 1)]
        return [part[2 * turn + 1, :, t_half(h)]] + [from_row[turn, k, :, t_half(h)] for k in range(row_n - 1)]

    def combined_logs(logs):
        highest = functools.reduce(jnp.maximum, logs)
        return highest + log2(sum(jnp.exp2(x - highest) for x in logs))

    def send_logs(h):
        at = s_half(h)
        shift_s[:, at] = along_lanes(s_ext[at, :], 3)
        found = jnp.sum(sums[:, at], axis=0, keepdims=True)
        logs = log2(found) - shift_s[:, at] * SCALE
        part[0, :, at] = jnp.where(found < 2.0**120, logs, jnp.nan)
        start("col", 0, h)

    for k in range(1, chips):
        s_copy(k).wait_recv()
        twin_copy(k).start()
        s_prepare(s_from(k))
    for j in range(1, per):
        t_copy(j).wait_recv()
    t_prepare([t_from(j) for j in range(1, per)])
    highs[...] = jnp.full_like(highs, -3e38)
    for k in range(chips):
        twin_copy(k).wait_recv()
        s_prepare(twin_from(k))

    def early(p, _):
        terms_with([t_from(per * p + j) for j in range(per)], 0)

        @pl.when(p < row_n // per - 1)
        def _():
            following = [per * p + per + j for j in range(per)]
            for k in following:
                t_copy(k).wait_recv()
            t_prepare([t_from(k) for k in following])

        return 0

    def late(p, _):
        terms_with([t_from(per * p + j) for j in range(per)], 1)
        return 0

    lax.fori_loop(0, row_n // per, early, 0)
    send_logs(0)
    lax.fori_loop(0, row_n // per, late, 0)
    send_logs(1)

    for k in range(1, chips):
        s_copy(k).wait_send()
    for k in range(chips):
        twin_copy(k).wait_send()
    for k in range(1, row_n):
        t_copy(k).wait_send()

    room = (FLOOR + math.log2(total_t) - CEIL) / SCALE

    def t_shift(i, _):
        size = min(512, nt)
        lane, ones = ones_at(size, 0)
        rows = pl.ds(pl.multiple_of(i * size, size), size)
        bias = jnp.sum(jnp.where(lane < 3, t_ext[rows, :].astype(F32), 0.0), axis=1, keepdims=True)
        shift = spread(bias - jnp.max(highs[rows, :], axis=1, keepdims=True) - room)
        t_ext[rows, :] = pick3(shift, lane, 3, ones)
        return 0

    t_sq[...] = -2.0 * along_lanes(t_ext[...], 0)
    lax.fori_loop(0, nt // min(512, nt), t_shift, 0)
    shift_t[...] = along_lanes(t_ext[...], 3)

    width = min(512, half_t)

    def second(h):
        def one(i, _):
            at = pl.ds(pl.multiple_of(i * width, width), width)
            rows = s_half(h)
            x = jnp.concatenate([s_all[rows, :], s_ext[rows, :]], axis=1)
            w = jnp.concatenate([t_all[at, :], t_ext[at, :]], axis=1)
            terms = jnp.exp2(nt_dot(x, w) * SCALE)
            kept[rows, at] = terms.astype(BF16)
            summed = jnp.sum(terms.reshape(half_s // 8, 8, width), axis=0)
            if h == 0:
                sums_t[:, at] = summed
            else:
                summed = jnp.sum(summed + sums_t[:, at], axis=0, keepdims=True)
                part[1, :, at] = log2(summed) - shift_t[:, at] * SCALE
            return 0

        return one

    for h in halves:
        at = s_half(h)
        f_ref[:, at] = math.log2(total_t) - combined_logs(finish("col", 0, h))

        def s_bias(i, _):
            size = min(512, half_s)
            lane, ones = ones_at(size, 3)
            rows = pl.ds(pl.multiple_of(i * size + h * half_s, size), size)
            bias = jnp.transpose(jnp.broadcast_to(f_ref[:, rows] * (1.0 / SCALE), (depth, size)))
            s_ext[rows, :] = pick3(bias, lane, 0, ones)
            return 0

        lax.fori_loop(0, half_s // min(512, half_s), s_bias, 0)
        if h == 0:
            lax.fori_loop(0, nt // width, second(h), 0)
    for h in halves:
        lax.fori_loop(h * half_t // width, (h + 1) * half_t // width, second(1), 0)
        start("row", 0, h)

    def s_norms(i, _):
        ones = jnp.full((16, depth), 1.0, BF16)
        rows = pl.ds(pl.multiple_of(i * own_s, own_s), own_s)
        x = s_all[rows, :].astype(F32)
        square = x * x
        high = square.astype(BF16)
        low = (square - high.astype(F32)).astype(BF16)
        s_sq[:, rows] = (nt_dot(ones, high) + nt_dot(ones, low))[0:1, :]
        return 0

    lax.fori_loop(0, col_n, s_norms, 0)

    size = min(512, half_s)
    fine = min(64, size)

    def row_sums(h, out):
        def one(i, _):
            for q in range(0, size, 128):
                pieces = []
                for r in range(q, q + 128, fine):
                    rows = pl.ds(pl.multiple_of(i * size, size) + r, fine)
                    summed = jnp.zeros((fine, 128), F32) if out is None else row_part[rows, :]
                    for c in range(h * half_t, (h + 1) * half_t, 128):
                        summed = summed + kept[rows, c : c + 128].astype(F32) * weight[1, :, c : c + 128]
                    if out is None:
                        row_part[rows, :] = summed
                    pieces.append(summed)
                if out is not None:
                    turned = jnp.transpose(jnp.concatenate(pieces, axis=0))
                    at = pl.ds(pl.multiple_of(i * size, size) + q, 128)
                    out[:, at] = jnp.sum(turned, axis=0, keepdims=True)
            return 0

        return one

    def col_sums(lhs, h, at):
        got = jnp.dot(lhs, kept[s_half(h), at], preferred_element_type=F32)
        return jnp.sum(got, axis=0, keepdims=True)

    def lhs_of(x):
        index = lax.broadcasted_iota(jnp.int32, (16, half_s), 0)
        return pick3(jnp.broadcast_to(x, (16, half_s)), index, 0, 0.0)

    for turn in range(1, ITERS + 1):
        for h in halves:
            at = t_half(h)
            arrived = finish("row", turn - 1, h)
            if turn == 1:
                logs = combined_logs(arrived)
                held = logs + shift_t[:, at] * SCALE
                g_ref[:, at] = jnp.where(held > -30.0, math.log2(total_s) - logs, jnp.nan)
                weight[0, :, at] = jnp.exp2(g_ref[:, at] - shift_t[:, at] * SCALE)
                weight[1, :, at] = weight[0, :, at]
            else:
                v = total_s / sum(arrived)
                if turn < ITERS:
                    weight[1, :, at] = weight[0, :, at] * v
                else:
                    g_ref[:, at] = BACK * (g_ref[:, at] + log2(v)) + t_sq[:, at]
            if turn < ITERS and h == 0:
                lax.fori_loop(0, ns // size, row_sums(0, None), 0)
        if turn == ITERS:
            break
        for h in halves:
            lax.fori_loop(h * half_s // size, (h + 1) * half_s // size, row_sums(1, part.at[2 * turn]), 0)
            start("col", turn, h)
        for h in halves:
            u = total_t / sum(finish("col", turn, h))
            if turn == ITERS - 1:
                f_ref[:, s_half(h)] = BACK * (f_ref[:, s_half(h)] + log2(u)) + s_sq[:, s_half(h)]
            lhs = lhs_of(u)
            for c in halves:
                at = t_half(c)
                got = col_sums(lhs, h, at)
                if h == 0:
                    col_part[:, at] = got
                else:
                    part[2 * turn + 1, :, at] = (got + col_part[:, at]) * weight[0, :, at]
                    start("row", turn, c)


def careful_kernel(
    row_n, col_n, s_ref, t_ref, f_ref, g_ref,
    s_all, t_all, s_ext, t_ext, kept, z0, z1, part, col_high, s_sq, t_sq, from_col, from_row,
    s_send, s_recv, t_send, t_recv, col_send, col_recv, row_send, row_recv,
):
    own_s, depth = s_ref.shape
    own_t = t_ref.shape[0]
    ns, nt = own_s * col_n, own_t * row_n
    total_s, total_t = float(ns * row_n), float(nt * col_n)
    my_row, my_col = lax.axis_index("row"), lax.axis_index("col")
    col_peers = [lax.rem(my_col + k, col_n) for k in range(1, col_n)]
    row_peers = [lax.rem(my_row + k, row_n) for k in range(1, row_n)]

    barrier = pltpu.get_barrier_semaphore()
    for peer in col_peers:
        pl.semaphore_signal(barrier, inc=1, device_id={"col": peer}, device_id_type=MESH)
    for peer in row_peers:
        pl.semaphore_signal(barrier, inc=1, device_id={"row": peer}, device_id_type=MESH)
    pl.semaphore_wait(barrier, col_n + row_n - 2)

    s_rows = pl.ds(pl.multiple_of(my_col * own_s, own_s), own_s)
    t_rows = pl.ds(pl.multiple_of(my_row * own_t, own_t), own_t)
    gathers = []
    for k, peer in enumerate(row_peers):
        gathers.append(
            pltpu.make_async_remote_copy(
                t_ref, t_all.at[t_rows, :], t_send.at[k], t_recv.at[k],
                device_id={"row": peer}, device_id_type=MESH,
            )
        )
    for k, peer in enumerate(col_peers):
        gathers.append(
            pltpu.make_async_remote_copy(
                s_ref, s_all.at[s_rows, :], s_send.at[k], s_recv.at[k],
                device_id={"col": peer}, device_id_type=MESH,
            )
        )
    for copy in gathers:
        copy.start()
    s_all[s_rows, :] = s_ref[...]
    t_all[t_rows, :] = t_ref[...]
    for copy in gathers:
        copy.wait()

    chunk = min(512, own_s, own_t)
    lane = lax.broadcasted_iota(jnp.int32, (chunk, depth), 1)
    ones = jnp.where(lane < 3, 1.0, 0.0).astype(BF16)

    def s_prepare(i, _):
        rows = pl.ds(pl.multiple_of(i * chunk, chunk), chunk)
        x = s_all[rows, :].astype(F32)
        s_sq[:, rows] = jnp.sum(jnp.transpose(x * x), axis=0, keepdims=True)
        s_ext[rows, :] = ones
        return 0

    def t_prepare(i, _):
        rows = pl.ds(pl.multiple_of(i * chunk, chunk), chunk)
        x = t_all[rows, :].astype(F32)
        t_sq[:, rows] = jnp.sum(jnp.transpose(x * x), axis=0, keepdims=True)
        bias = jnp.sum(x * x, axis=1, keepdims=True) * -0.5
        t_ext[rows, :] = pick3(jnp.broadcast_to(bias, (chunk, depth)), lane, 0, 0.0)
        return 0

    lax.fori_loop(0, ns // chunk, s_prepare, 0)
    lax.fori_loop(0, nt // chunk, t_prepare, 0)

    def logs_pass(x_all, x_ext, w_all, w_ext, out, keep):
        nx, nw = x_all.shape[0], w_all.shape[0]
        width = z0.shape[1]
        tiles = nw // width
        step = min(512, nx)
        fine = min(64, step)

        def lanes(tile):
            return pl.ds(pl.multiple_of(tile * width, width), width)

        def scores(tile, q, z, highest):
            rows = pl.ds(q * step, step)
            at = lanes(tile)
            x = jnp.concatenate([x_all[rows, :], x_ext[rows, :]], axis=1)
            w = jnp.concatenate([w_all[at, :], w_ext[at, :]], axis=1)
            inner = nt_dot(x, w)
            z[rows, :] = inner
            return jnp.maximum(highest, jnp.max(inner.reshape(step // 8, 8, width), axis=0))

        def sums(tile, q, z, highest, summed):
            for j in range(q * step, (q + 1) * step, fine):
                rows = pl.ds(j, fine)
                shifted = z[rows, :].reshape(fine // 8, 8, width) - highest[None]
                terms = jnp.exp2(shifted * SCALE)
                if keep:
                    kept[rows, lanes(tile)] = terms.reshape(fine, width).astype(BF16)
                summed = summed + jnp.sum(terms, axis=0)
            return summed

        def settle(highest):
            return jnp.broadcast_to(jnp.max(highest, axis=0, keepdims=True), (8, width))

        low = jnp.full((8, width), -3e38, F32)

        def both(tile, z_now, highest, z_next):
            following = jnp.minimum(tile + 1, tiles - 1)
            new_high = low
            summed = jnp.zeros((8, width), F32)
            for q in range(nx // step):
                new_high = scores(following, q, z_next, new_high)
                summed = sums(tile, q, z_now, highest, summed)
            top = highest[0:1, :] * SCALE
            out[:, lanes(tile)] = top + log2(jnp.sum(summed, axis=0, keepdims=True))
            if keep:
                col_high[:, lanes(tile)] = top
            return settle(new_high)

        def pair(i, highest):
            highest = both(2 * i, z0, highest, z1)
            return both(2 * i + 1, z1, highest, z0)

        first = low
        for q in range(nx // step):
            first = scores(0, q, z0, first)
        lax.fori_loop(0, tiles // 2, pair, settle(first))

    def exchange(turn, sent, received, send, recv, axis, peers):
        copies = [
            pltpu.make_async_remote_copy(
                sent, received.at[turn, k], send.at[turn, k], recv.at[turn, k],
                device_id={axis: peer}, device_id_type=MESH,
            )
            for k, peer in enumerate(peers)
        ]
        for copy in copies:
            copy.start()
        for copy in copies:
            copy.wait()
        return [sent[...]] + [received[turn, k] for k in range(len(peers))]

    def over_col(turn):
        return exchange(turn, part.at[2 * turn], from_col, col_send, col_recv, "col", col_peers)

    def over_row(turn):
        return exchange(turn, part.at[2 * turn + 1], from_row, row_send, row_recv, "row", row_peers)

    def combined_logs(logs):
        highest = functools.reduce(jnp.maximum, logs)
        return highest + log2(sum(jnp.exp2(x - highest) for x in logs))

    logs_pass(t_all, t_ext, s_all, s_ext, part.at[0], False)
    f_first = math.log2(total_t) - combined_logs(over_col(0))
    f_ref[...] = f_first

    def s_bias(i, _):
        rows = pl.ds(pl.multiple_of(i * chunk, chunk), chunk)
        bias = jnp.transpose(jnp.broadcast_to(f_ref[:, rows] * (1.0 / SCALE), (depth, chunk)))
        s_ext[rows, :] = pick3(bias, lane, 0, 0.0)
        return 0

    def t_ones(i, _):
        t_ext[pl.ds(pl.multiple_of(i * chunk, chunk), chunk), :] = ones
        return 0

    lax.fori_loop(0, ns // chunk, s_bias, 0)
    lax.fori_loop(0, nt // chunk, t_ones, 0)
    logs_pass(s_all, s_ext, t_all, t_ext, part.at[1], True)
    g_first = math.log2(total_s) - combined_logs(over_row(0))
    g_ref[...] = g_first
    col_high[...] = jnp.exp2(g_first + col_high[...])

    block = min(512, ns, nt)

    def parts_of(x):
        index = lax.broadcasted_iota(jnp.int32, (16, x.shape[1]), 0)
        return pick3(jnp.broadcast_to(x, (16, x.shape[1])), index, 0, 0.0)

    def row_sums(x, out):
        lhs = parts_of(x)

        def one(i, _):
            rows = pl.ds(pl.multiple_of(i * block, block), block)
            out[:, rows] = jnp.sum(nt_dot(lhs, kept[rows, :]), axis=0, keepdims=True)
            return 0

        lax.fori_loop(0, ns // block, one, 0)

    def col_sums(x, out):
        lhs = parts_of(x)

        def one(i, _):
            at = pl.ds(pl.multiple_of(i * block, block), block)
            found = jnp.dot(lhs, kept[:, at], preferred_element_type=F32)
            out[:, at] = jnp.sum(found, axis=0, keepdims=True) * col_high[:, at]
            return 0

        lax.fori_loop(0, nt // block, one, 0)

    weight = col_high[...]
    for turn in range(1, ITERS):
        row_sums(weight, part.at[2 * turn])
        u = total_t / sum(over_col(turn))
        col_sums(u, part.at[2 * turn + 1])
        v = total_s / sum(over_row(turn))
        weight = col_high[...] * v
    f_ref[...] = BACK * (f_ref[...] + log2(u)) + s_sq[...]
    g_ref[...] = BACK * (g_ref[...] + log2(v)) + t_sq[...]


def careful(row_n, col_n, source, target):
    own_s, depth = source.shape
    own_t = target.shape[0]
    ns, nt = own_s * col_n, own_t * row_n
    width = min(256, ns // 2, nt // 2)
    vmem = pl.BlockSpec(memory_space=pltpu.VMEM)
    dma = pltpu.SemaphoreType.DMA
    f, g = pl.pallas_call(
        functools.partial(careful_kernel, row_n, col_n),
        out_shape=(jax.ShapeDtypeStruct((1, ns), F32), jax.ShapeDtypeStruct((1, nt), F32)),
        in_specs=[vmem, vmem],
        out_specs=(vmem, vmem),
        scratch_shapes=[
            pltpu.VMEM((ns, depth), BF16),
            pltpu.VMEM((nt, depth), BF16),
            pltpu.VMEM((ns, depth), BF16),
            pltpu.VMEM((nt, depth), BF16),
            pltpu.VMEM((ns, nt), BF16),
            pltpu.VMEM((max(ns, nt), width), F32),
            pltpu.VMEM((max(ns, nt), width), F32),
            pltpu.VMEM((2 * ITERS, 1, max(ns, nt)), F32),
            pltpu.VMEM((1, nt), F32),
            pltpu.VMEM((1, ns), F32),
            pltpu.VMEM((1, nt), F32),
            pltpu.VMEM((ITERS, col_n - 1, 1, ns), F32),
            pltpu.VMEM((ITERS, row_n - 1, 1, nt), F32),
            dma((col_n - 1,)),
            dma((col_n - 1,)),
            dma((row_n - 1,)),
            dma((row_n - 1,)),
            dma((ITERS, col_n - 1)),
            dma((ITERS, col_n - 1)),
            dma((ITERS, row_n - 1)),
            dma((ITERS, row_n - 1)),
        ],
        compiler_params=pltpu.CompilerParams(
            collective_id=1, has_side_effects=True, vmem_limit_bytes=60 << 20
        ),
        cost_estimate=pl.CostEstimate(
            flops=12 * ns * nt * depth, bytes_accessed=2 * (ns + nt) * depth, transcendentals=2 * ns * nt
        ),
    )(source, target)
    return f.reshape(ns), g.reshape(nt)


def on_device(row_n, col_n, source, target):
    own_s, depth = source.shape
    own_t = target.shape[0]
    ns, nt = own_s * col_n, own_t * row_n
    vmem = pl.BlockSpec(memory_space=pltpu.VMEM)
    dma = pltpu.SemaphoreType.DMA
    f, g = pl.pallas_call(
        functools.partial(kernel, row_n, col_n),
        out_shape=(jax.ShapeDtypeStruct((1, ns), F32), jax.ShapeDtypeStruct((1, nt), F32)),
        in_specs=[vmem, vmem],
        out_specs=(vmem, vmem),
        scratch_shapes=[
            pltpu.VMEM((ns, depth), BF16),
            pltpu.VMEM((nt, depth), BF16),
            pltpu.VMEM((ns, depth), BF16),
            pltpu.VMEM((nt, depth), BF16),
            pltpu.VMEM((ns, nt), BF16),
            pltpu.VMEM((8, ns), F32),
            pltpu.VMEM((8, nt), F32),
            pltpu.VMEM((nt, depth), F32),
            pltpu.VMEM((ns, 128), F32),
            pltpu.VMEM((1, nt), F32),
            pltpu.VMEM((2 * ITERS, 1, max(ns, nt)), F32),
            pltpu.VMEM((2, 1, nt), F32),
            pltpu.VMEM((1, ns), F32),
            pltpu.VMEM((1, nt), F32),
            pltpu.VMEM((1, ns), F32),
            pltpu.VMEM((1, nt), F32),
            pltpu.VMEM((ITERS, col_n - 1, 1, ns), F32),
            pltpu.VMEM((ITERS, row_n - 1, 1, nt), F32),
            dma((col_n // 2,)),
            dma((col_n // 2,)),
            dma((row_n,)),
            dma((row_n,)),
            dma((col_n // 2,)),
            dma((col_n // 2,)),
            dma((ITERS, 2, col_n - 1)),
            dma((ITERS, 2, col_n - 1)),
            dma((ITERS, 2, row_n - 1)),
            dma((ITERS, 2, row_n - 1)),
        ],
        compiler_params=pltpu.CompilerParams(
            collective_id=0, has_side_effects=True, vmem_limit_bytes=60 << 20
        ),
        cost_estimate=pl.CostEstimate(
            flops=12 * ns * nt * depth, bytes_accessed=2 * (ns + nt) * depth, transcendentals=2 * ns * nt
        ),
    )(source, target)
    fast = f.reshape(ns), g.reshape(nt)
    return lax.cond(jnp.isnan(f[0, 0]), lambda: careful(row_n, col_n, source, target), lambda: fast)


def solution(mesh):
    placed = (P(("row", "col"), None), P(("col", "row"), None))
    return jax.shard_map(
        functools.partial(on_device, mesh.shape["row"], mesh.shape["col"]),
        mesh=mesh,
        in_specs=placed,
        out_specs=(P("row"), P("col")),
        check_vma=False,
    )
```

```python
import functools
import math

import jax
import jax.numpy as jnp
from jax import lax
from jax.experimental import pallas as pl
from jax.experimental.pallas import tpu as pltpu
from jax.sharding import PartitionSpec as P

ITERS = 3
EPS = 0.02
LOG2E = 1.0 / math.log(2.0)
SCALE = 2.0 * LOG2E / EPS
BACK = EPS / LOG2E
FLOOR = 90.0
CEIL = 100.0
F32 = jnp.float32
BF16 = jnp.bfloat16
MESH = pl.DeviceIdType.MESH


def log2(x):
    return jnp.log(x) * LOG2E


def split3(x):
    high = x.astype(BF16).astype(F32)
    mid = (x - high).astype(BF16).astype(F32)
    return high, mid, x - high - mid


def pick3(x, index, base, other):
    high, mid, low = split3(x)
    found = jnp.where(index == base + 1, mid, jnp.where(index == base + 2, low, other))
    return jnp.where(index == base, high, found).astype(BF16)


def nt_dot(x, y):
    return lax.dot_general(x, y, (((1,), (1,)), ((), ())), preferred_element_type=F32)


def kernel(
    row_n, col_n, s_ref, t_ref, f_ref, g_ref,
    s_all, t_all, s_ext, t_ext, kept, sums, sums_t, highs, row_part, col_part, part, weight, s_sq, t_sq, shift_s, shift_t,
    from_col, from_row,
    s_send, s_recv, t_send, t_recv, pair_send, pair_recv, col_send, col_recv, row_send, row_recv,
):
    own_s, depth = s_ref.shape
    own_t = t_ref.shape[0]
    ns, nt = own_s * col_n, own_t * row_n
    total_s, total_t = float(ns * row_n), float(nt * col_n)
    my_row, my_col = lax.axis_index("row"), lax.axis_index("col")
    col_peers = [lax.rem(my_col + k, col_n) for k in range(1, col_n)]
    row_peers = [lax.rem(my_row + k, row_n) for k in range(1, row_n)]
    my_core = lax.rem(my_col, 2)
    twin = my_col + 1 - 2 * my_core
    chips = col_n // 2

    barrier = pltpu.get_barrier_semaphore()
    for peer in col_peers:
        pl.semaphore_signal(barrier, inc=1, device_id={"col": peer}, device_id_type=MESH)
    for peer in row_peers:
        pl.semaphore_signal(barrier, inc=1, device_id={"row": peer}, device_id_type=MESH)

    def s_block(index):
        return pl.ds(pl.multiple_of(index * own_s, own_s), own_s)

    def t_block(index):
        return pl.ds(pl.multiple_of(index * own_t, own_t), own_t)

    def s_from(k):
        return lax.rem(my_col - 2 * k + col_n, col_n)

    def twin_from(k):
        return lax.rem(twin - 2 * k + col_n, col_n)

    side = math.isqrt(row_n)
    my_z, my_x = my_row // side, my_row % side

    def away(k):
        z, x = 2 * (k // 8) + (k // 2) % 2, 2 * ((k // 4) % 2) + k % 2
        return z + z // 2 - 2 * (z // 3), x + x // 2 - 2 * (x // 3)

    def t_from(k):
        z, x = away(k)
        return (my_z - z + side) % side * side + (my_x - x + side) % side

    def t_to(k):
        z, x = away(k)
        return (my_z + z) % side * side + (my_x + x) % side

    waves = [[k for k in wave if k < row_n] for wave in ((1, 2, 3, 4, 8), (5, 6, 7, 9, 10), (11, 12, 13, 14, 15))]

    def t_copy(k):
        return pltpu.make_async_remote_copy(
            t_ref, t_all.at[t_block(my_row), :], t_send.at[k], t_recv.at[k],
            device_id={"row": t_to(k)}, device_id_type=MESH,
        )

    def s_copy(k):
        return pltpu.make_async_remote_copy(
            s_ref, s_all.at[s_block(my_col), :], s_send.at[k], s_recv.at[k],
            device_id={"col": lax.rem(my_col + 2 * k, col_n)}, device_id_type=MESH,
        )

    def twin_copy(k):
        at = s_all.at[s_block(s_from(k)), :]
        return pltpu.make_async_remote_copy(
            s_ref if k == 0 else at, at, pair_send.at[k], pair_recv.at[k], device_id={"col": twin}, device_id_type=MESH
        )

    pl.semaphore_wait(barrier, col_n + row_n - 2)
    for k in range(1, chips):
        s_copy(k).start()
    twin_copy(0).start()
    for k in waves[0]:
        t_copy(k).start()

    chunk = 128

    def ones_at(rows, first):
        lane = lax.broadcasted_iota(jnp.int32, (rows, depth), 1)
        return lane, jnp.where((lane >= first) & (lane < first + 3), 1.0, 0.0)

    def spread(column):
        return jnp.broadcast_to(column, (column.shape[0], depth))

    def along_lanes(ext, first):
        select = ones_at(16, first)[1].astype(BF16)
        return nt_dot(select, ext)[0:1, :]

    def t_prepare(index):
        lane, ones = ones_at(own_t, 3)
        for i in index:
            x = t_all[t_block(i), :].astype(F32)
            bias = spread(jnp.sum(x * x, axis=1, keepdims=True) * -0.5)
            t_ext[t_block(i), :] = pick3(bias, lane, 0, ones)

    def s_prepare(i):
        lane, ones = ones_at(own_s, 0)
        sample = jnp.concatenate([t_ref[...], t_ext[t_block(my_row), :]], axis=1)
        x = jnp.concatenate([s_all[s_block(i), :], ones.astype(BF16)], axis=1)
        shift = spread(-FLOOR / SCALE - jnp.max(nt_dot(x, sample), axis=1, keepdims=True))
        s_ext[s_block(i), :] = pick3(shift, lane, 3, ones)

    s_all[s_block(my_col), :] = s_ref[...]
    t_all[t_block(my_row), :] = t_ref[...]
    sums[...] = jnp.zeros_like(sums)
    t_prepare([my_row])
    s_prepare(my_col)

    per = 2
    half_s, half_t = ns // 2, nt // 2
    halves = (0, 1)

    def s_half(h):
        return pl.ds(h * half_s, half_s)

    def t_half(h):
        return pl.ds(h * half_t, half_t)

    def terms_with(t_index, h):
        x = jnp.concatenate(
            [jnp.concatenate([t_all[t_block(i), :], t_ext[t_block(i), :]], axis=1) for i in t_index], axis=0
        )
        high = None
        for i in range(h * col_n // 2, (h + 1) * col_n // 2):
            at = pl.ds(i * own_s, own_s)
            z = nt_dot(x, jnp.concatenate([s_all[at, :], s_ext[at, :]], axis=1))
            for c in range(0, own_s, depth):
                piece = z[:, c : c + depth]
                high = piece if high is None else jnp.maximum(high, piece)
            terms = jnp.exp2(z * SCALE).reshape(z.shape[0] // 8, 8, own_s)
            sums[:, at] = sums[:, at] + jnp.sum(terms, axis=0)
        for n, i in enumerate(t_index):
            at = t_block(i)
            highs[at, :] = jnp.maximum(highs[at, :], high[n * own_t : (n + 1) * own_t, :])

    def over(axis, turn, h):
        if axis == "col":
            here, there, send, recv, peers, at = part.at[2 * turn], from_col, col_send, col_recv, col_peers, s_half(h)
        else:
            here, there, send, recv, peers, at = part.at[2 * turn + 1], from_row, row_send, row_recv, row_peers, t_half(h)
        return [
            pltpu.make_async_remote_copy(
                here.at[:, at], there.at[turn, k, :, at], send.at[turn, h, k], recv.at[turn, h, k],
                device_id={axis: peer}, device_id_type=MESH,
            )
            for k, peer in enumerate(peers)
        ]

    def start(axis, turn, h):
        for copy in over(axis, turn, h):
            copy.start()

    def finish(axis, turn, h):
        for copy in over(axis, turn, h):
            copy.wait()
        if axis == "col":
            return [part[2 * turn, :, s_half(h)]] + [from_col[turn, k, :, s_half(h)] for k in range(col_n - 1)]
        return [part[2 * turn + 1, :, t_half(h)]] + [from_row[turn, k, :, t_half(h)] for k in range(row_n - 1)]

    def combined_logs(logs):
        highest = functools.reduce(jnp.maximum, logs)
        return highest + log2(sum(jnp.exp2(x - highest) for x in logs))

    def send_logs(h):
        at = s_half(h)
        shift_s[:, at] = along_lanes(s_ext[at, :], 3)
        found = jnp.sum(sums[:, at], axis=0, keepdims=True)
        logs = log2(found) - shift_s[:, at] * SCALE
        part[0, :, at] = jnp.where(found < 2.0**120, logs, jnp.nan)
        start("col", 0, h)

    for before, wave in zip(waves, waves[1:]):
        for k in before:
            t_copy(k).wait_send()
        for k in wave:
            t_copy(k).start()
        if before is waves[0]:
            for j in range(1, per):
                t_copy(j).wait_recv()
            t_prepare([t_from(j) for j in range(1, per)])
            highs[...] = jnp.full_like(highs, -3e38)
    for k in range(1, chips):
        s_copy(k).wait_recv()
        twin_copy(k).start()
        s_prepare(s_from(k))
    for k in range(chips):
        twin_copy(k).wait_recv()
        s_prepare(twin_from(k))

    def early(p, _):
        terms_with([t_from(per * p + j) for j in range(per)], 0)

        @pl.when(p < row_n // per - 1)
        def _():
            following = [per * p + per + j for j in range(per)]
            for k in following:
                t_copy(k).wait_recv()
            t_prepare([t_from(k) for k in following])

        return 0

    def late(p, _):
        terms_with([t_from(per * p + j) for j in range(per)], 1)
        return 0

    lax.fori_loop(0, row_n // per, early, 0)
    send_logs(0)
    lax.fori_loop(0, row_n // per, late, 0)
    send_logs(1)

    for k in range(1, chips):
        s_copy(k).wait_send()
    for k in range(chips):
        twin_copy(k).wait_send()
    for k in waves[2]:
        t_copy(k).wait_send()

    room = (FLOOR + math.log2(total_t) - CEIL) / SCALE

    def t_shift(i, _):
        size = min(512, nt)
        lane, ones = ones_at(size, 0)
        rows = pl.ds(pl.multiple_of(i * size, size), size)
        bias = jnp.sum(jnp.where(lane < 3, t_ext[rows, :].astype(F32), 0.0), axis=1, keepdims=True)
        shift = spread(bias - jnp.max(highs[rows, :], axis=1, keepdims=True) - room)
        t_ext[rows, :] = pick3(shift, lane, 3, ones)
        return 0

    t_sq[...] = -2.0 * along_lanes(t_ext[...], 0)
    lax.fori_loop(0, nt // min(512, nt), t_shift, 0)
    shift_t[...] = along_lanes(t_ext[...], 3)

    width = min(512, half_t)

    def second(h):
        def one(i, _):
            at = pl.ds(pl.multiple_of(i * width, width), width)
            rows = s_half(h)
            x = jnp.concatenate([s_all[rows, :], s_ext[rows, :]], axis=1)
            w = jnp.concatenate([t_all[at, :], t_ext[at, :]], axis=1)
            terms = jnp.exp2(nt_dot(x, w) * SCALE)
            kept[rows, at] = terms.astype(BF16)
            summed = jnp.sum(terms.reshape(half_s // 8, 8, width), axis=0)
            if h == 0:
                sums_t[:, at] = summed
            else:
                summed = jnp.sum(summed + sums_t[:, at], axis=0, keepdims=True)
                part[1, :, at] = log2(summed) - shift_t[:, at] * SCALE
            return 0

        return one

    for h in halves:
        at = s_half(h)
        f_ref[:, at] = math.log2(total_t) - combined_logs(finish("col", 0, h))

        def s_bias(i, _):
            size = min(512, half_s)
            lane, ones = ones_at(size, 3)
            rows = pl.ds(pl.multiple_of(i * size + h * half_s, size), size)
            bias = jnp.transpose(jnp.broadcast_to(f_ref[:, rows] * (1.0 / SCALE), (depth, size)))
            s_ext[rows, :] = pick3(bias, lane, 0, ones)
            return 0

        lax.fori_loop(0, half_s // min(512, half_s), s_bias, 0)
        if h == 0:
            lax.fori_loop(0, nt // width, second(h), 0)
    for h in halves:
        lax.fori_loop(h * half_t // width, (h + 1) * half_t // width, second(1), 0)
        start("row", 0, h)

    def s_norms(i, _):
        ones = jnp.full((16, depth), 1.0, BF16)
        rows = pl.ds(pl.multiple_of(i * own_s, own_s), own_s)
        x = s_all[rows, :].astype(F32)
        square = x * x
        high = square.astype(BF16)
        low = (square - high.astype(F32)).astype(BF16)
        s_sq[:, rows] = (nt_dot(ones, high) + nt_dot(ones, low))[0:1, :]
        return 0

    lax.fori_loop(0, col_n, s_norms, 0)

    size = min(512, half_s)
    fine = min(64, size)

    def row_sums(h, out):
        def one(i, _):
            for q in range(0, size, 128):
                pieces = []
                for r in range(q, q + 128, fine):
                    rows = pl.ds(pl.multiple_of(i * size, size) + r, fine)
                    summed = jnp.zeros((fine, 128), F32) if out is None else row_part[rows, :]
                    for c in range(h * half_t, (h + 1) * half_t, 128):
                        summed = summed + kept[rows, c : c + 128].astype(F32) * weight[1, :, c : c + 128]
                    if out is None:
                        row_part[rows, :] = summed
                    pieces.append(summed)
                if out is not None:
                    turned = jnp.transpose(jnp.concatenate(pieces, axis=0))
                    at = pl.ds(pl.multiple_of(i * size, size) + q, 128)
                    out[:, at] = jnp.sum(turned, axis=0, keepdims=True)
            return 0

        return one

    def col_sums(lhs, h, at):
        got = jnp.dot(lhs, kept[s_half(h), at], preferred_element_type=F32)
        return jnp.sum(got, axis=0, keepdims=True)

    def lhs_of(x):
        index = lax.broadcasted_iota(jnp.int32, (16, half_s), 0)
        return pick3(jnp.broadcast_to(x, (16, half_s)), index, 0, 0.0)

    for turn in range(1, ITERS + 1):
        for h in halves:
            at = t_half(h)
            arrived = finish("row", turn - 1, h)
            if turn == 1:
                logs = combined_logs(arrived)
                held = logs + shift_t[:, at] * SCALE
                g_ref[:, at] = jnp.where(held > -30.0, math.log2(total_s) - logs, jnp.nan)
                weight[0, :, at] = jnp.exp2(g_ref[:, at] - shift_t[:, at] * SCALE)
                weight[1, :, at] = weight[0, :, at]
            else:
                v = total_s / sum(arrived)
                if turn < ITERS:
                    weight[1, :, at] = weight[0, :, at] * v
                else:
                    g_ref[:, at] = BACK * (g_ref[:, at] + log2(v)) + t_sq[:, at]
            if turn < ITERS and h == 0:
                lax.fori_loop(0, ns // size, row_sums(0, None), 0)
        if turn == ITERS:
            break
        for h in halves:
            lax.fori_loop(h * half_s // size, (h + 1) * half_s // size, row_sums(1, part.at[2 * turn]), 0)
            start("col", turn, h)
        for h in halves:
            u = total_t / sum(finish("col", turn, h))
            if turn == ITERS - 1:
                f_ref[:, s_half(h)] = BACK * (f_ref[:, s_half(h)] + log2(u)) + s_sq[:, s_half(h)]
            lhs = lhs_of(u)
            for c in halves:
                at = t_half(c)
                got = col_sums(lhs, h, at)
                if h == 0:
                    col_part[:, at] = got
                else:
                    part[2 * turn + 1, :, at] = (got + col_part[:, at]) * weight[0, :, at]
                    start("row", turn, c)


def careful_kernel(
    row_n, col_n, s_ref, t_ref, f_ref, g_ref,
    s_all, t_all, s_ext, t_ext, kept, z0, z1, part, col_high, s_sq, t_sq, from_col, from_row,
    s_send, s_recv, t_send, t_recv, col_send, col_recv, row_send, row_recv,
):
    own_s, depth = s_ref.shape
    own_t = t_ref.shape[0]
    ns, nt = own_s * col_n, own_t * row_n
    total_s, total_t = float(ns * row_n), float(nt * col_n)
    my_row, my_col = lax.axis_index("row"), lax.axis_index("col")
    col_peers = [lax.rem(my_col + k, col_n) for k in range(1, col_n)]
    row_peers = [lax.rem(my_row + k, row_n) for k in range(1, row_n)]

    barrier = pltpu.get_barrier_semaphore()
    for peer in col_peers:
        pl.semaphore_signal(barrier, inc=1, device_id={"col": peer}, device_id_type=MESH)
    for peer in row_peers:
        pl.semaphore_signal(barrier, inc=1, device_id={"row": peer}, device_id_type=MESH)
    pl.semaphore_wait(barrier, col_n + row_n - 2)

    s_rows = pl.ds(pl.multiple_of(my_col * own_s, own_s), own_s)
    t_rows = pl.ds(pl.multiple_of(my_row * own_t, own_t), own_t)
    gathers = []
    for k, peer in enumerate(row_peers):
        gathers.append(
            pltpu.make_async_remote_copy(
                t_ref, t_all.at[t_rows, :], t_send.at[k], t_recv.at[k],
                device_id={"row": peer}, device_id_type=MESH,
            )
        )
    for k, peer in enumerate(col_peers):
        gathers.append(
            pltpu.make_async_remote_copy(
                s_ref, s_all.at[s_rows, :], s_send.at[k], s_recv.at[k],
                device_id={"col": peer}, device_id_type=MESH,
            )
        )
    for copy in gathers:
        copy.start()
    s_all[s_rows, :] = s_ref[...]
    t_all[t_rows, :] = t_ref[...]
    for copy in gathers:
        copy.wait()

    chunk = min(512, own_s, own_t)
    lane = lax.broadcasted_iota(jnp.int32, (chunk, depth), 1)
    ones = jnp.where(lane < 3, 1.0, 0.0).astype(BF16)

    def s_prepare(i, _):
        rows = pl.ds(pl.multiple_of(i * chunk, chunk), chunk)
        x = s_all[rows, :].astype(F32)
        s_sq[:, rows] = jnp.sum(jnp.transpose(x * x), axis=0, keepdims=True)
        s_ext[rows, :] = ones
        return 0

    def t_prepare(i, _):
        rows = pl.ds(pl.multiple_of(i * chunk, chunk), chunk)
        x = t_all[rows, :].astype(F32)
        t_sq[:, rows] = jnp.sum(jnp.transpose(x * x), axis=0, keepdims=True)
        bias = jnp.sum(x * x, axis=1, keepdims=True) * -0.5
        t_ext[rows, :] = pick3(jnp.broadcast_to(bias, (chunk, depth)), lane, 0, 0.0)
        return 0

    lax.fori_loop(0, ns // chunk, s_prepare, 0)
    lax.fori_loop(0, nt // chunk, t_prepare, 0)

    def logs_pass(x_all, x_ext, w_all, w_ext, out, keep):
        nx, nw = x_all.shape[0], w_all.shape[0]
        width = z0.shape[1]
        tiles = nw // width
        step = min(512, nx)
        fine = min(64, step)

        def lanes(tile):
            return pl.ds(pl.multiple_of(tile * width, width), width)

        def scores(tile, q, z, highest):
            rows = pl.ds(q * step, step)
            at = lanes(tile)
            x = jnp.concatenate([x_all[rows, :], x_ext[rows, :]], axis=1)
            w = jnp.concatenate([w_all[at, :], w_ext[at, :]], axis=1)
            inner = nt_dot(x, w)
            z[rows, :] = inner
            return jnp.maximum(highest, jnp.max(inner.reshape(step // 8, 8, width), axis=0))

        def sums(tile, q, z, highest, summed):
            for j in range(q * step, (q + 1) * step, fine):
                rows = pl.ds(j, fine)
                shifted = z[rows, :].reshape(fine // 8, 8, width) - highest[None]
                terms = jnp.exp2(shifted * SCALE)
                if keep:
                    kept[rows, lanes(tile)] = terms.reshape(fine, width).astype(BF16)
                summed = summed + jnp.sum(terms, axis=0)
            return summed

        def settle(highest):
            return jnp.broadcast_to(jnp.max(highest, axis=0, keepdims=True), (8, width))

        low = jnp.full((8, width), -3e38, F32)

        def both(tile, z_now, highest, z_next):
            following = jnp.minimum(tile + 1, tiles - 1)
            new_high = low
            summed = jnp.zeros((8, width), F32)
            for q in range(nx // step):
                new_high = scores(following, q, z_next, new_high)
                summed = sums(tile, q, z_now, highest, summed)
            top = highest[0:1, :] * SCALE
            out[:, lanes(tile)] = top + log2(jnp.sum(summed, axis=0, keepdims=True))
            if keep:
                col_high[:, lanes(tile)] = top
            return settle(new_high)

        def pair(i, highest):
            highest = both(2 * i, z0, highest, z1)
            return both(2 * i + 1, z1, highest, z0)

        first = low
        for q in range(nx // step):
            first = scores(0, q, z0, first)
        lax.fori_loop(0, tiles // 2, pair, settle(first))

    def exchange(turn, sent, received, send, recv, axis, peers):
        copies = [
            pltpu.make_async_remote_copy(
                sent, received.at[turn, k], send.at[turn, k], recv.at[turn, k],
                device_id={axis: peer}, device_id_type=MESH,
            )
            for k, peer in enumerate(peers)
        ]
        for copy in copies:
            copy.start()
        for copy in copies:
            copy.wait()
        return [sent[...]] + [received[turn, k] for k in range(len(peers))]

    def over_col(turn):
        return exchange(turn, part.at[2 * turn], from_col, col_send, col_recv, "col", col_peers)

    def over_row(turn):
        return exchange(turn, part.at[2 * turn + 1], from_row, row_send, row_recv, "row", row_peers)

    def combined_logs(logs):
        highest = functools.reduce(jnp.maximum, logs)
        return highest + log2(sum(jnp.exp2(x - highest) for x in logs))

    logs_pass(t_all, t_ext, s_all, s_ext, part.at[0], False)
    f_first = math.log2(total_t) - combined_logs(over_col(0))
    f_ref[...] = f_first

    def s_bias(i, _):
        rows = pl.ds(pl.multiple_of(i * chunk, chunk), chunk)
        bias = jnp.transpose(jnp.broadcast_to(f_ref[:, rows] * (1.0 / SCALE), (depth, chunk)))
        s_ext[rows, :] = pick3(bias, lane, 0, 0.0)
        return 0

    def t_ones(i, _):
        t_ext[pl.ds(pl.multiple_of(i * chunk, chunk), chunk), :] = ones
        return 0

    lax.fori_loop(0, ns // chunk, s_bias, 0)
    lax.fori_loop(0, nt // chunk, t_ones, 0)
    logs_pass(s_all, s_ext, t_all, t_ext, part.at[1], True)
    g_first = math.log2(total_s) - combined_logs(over_row(0))
    g_ref[...] = g_first
    col_high[...] = jnp.exp2(g_first + col_high[...])

    block = min(512, ns, nt)

    def parts_of(x):
        index = lax.broadcasted_iota(jnp.int32, (16, x.shape[1]), 0)
        return pick3(jnp.broadcast_to(x, (16, x.shape[1])), index, 0, 0.0)

    def row_sums(x, out):
        lhs = parts_of(x)

        def one(i, _):
            rows = pl.ds(pl.multiple_of(i * block, block), block)
            out[:, rows] = jnp.sum(nt_dot(lhs, kept[rows, :]), axis=0, keepdims=True)
            return 0

        lax.fori_loop(0, ns // block, one, 0)

    def col_sums(x, out):
        lhs = parts_of(x)

        def one(i, _):
            at = pl.ds(pl.multiple_of(i * block, block), block)
            found = jnp.dot(lhs, kept[:, at], preferred_element_type=F32)
            out[:, at] = jnp.sum(found, axis=0, keepdims=True) * col_high[:, at]
            return 0

        lax.fori_loop(0, nt // block, one, 0)

    weight = col_high[...]
    for turn in range(1, ITERS):
        row_sums(weight, part.at[2 * turn])
        u = total_t / sum(over_col(turn))
        col_sums(u, part.at[2 * turn + 1])
        v = total_s / sum(over_row(turn))
        weight = col_high[...] * v
    f_ref[...] = BACK * (f_ref[...] + log2(u)) + s_sq[...]
    g_ref[...] = BACK * (g_ref[...] + log2(v)) + t_sq[...]


def careful(row_n, col_n, source, target):
    own_s, depth = source.shape
    own_t = target.shape[0]
    ns, nt = own_s * col_n, own_t * row_n
    width = min(256, ns // 2, nt // 2)
    vmem = pl.BlockSpec(memory_space=pltpu.VMEM)
    dma = pltpu.SemaphoreType.DMA
    f, g = pl.pallas_call(
        functools.partial(careful_kernel, row_n, col_n),
        out_shape=(jax.ShapeDtypeStruct((1, ns), F32), jax.ShapeDtypeStruct((1, nt), F32)),
        in_specs=[vmem, vmem],
        out_specs=(vmem, vmem),
        scratch_shapes=[
            pltpu.VMEM((ns, depth), BF16),
            pltpu.VMEM((nt, depth), BF16),
            pltpu.VMEM((ns, depth), BF16),
            pltpu.VMEM((nt, depth), BF16),
            pltpu.VMEM((ns, nt), BF16),
            pltpu.VMEM((max(ns, nt), width), F32),
            pltpu.VMEM((max(ns, nt), width), F32),
            pltpu.VMEM((2 * ITERS, 1, max(ns, nt)), F32),
            pltpu.VMEM((1, nt), F32),
            pltpu.VMEM((1, ns), F32),
            pltpu.VMEM((1, nt), F32),
            pltpu.VMEM((ITERS, col_n - 1, 1, ns), F32),
            pltpu.VMEM((ITERS, row_n - 1, 1, nt), F32),
            dma((col_n - 1,)),
            dma((col_n - 1,)),
            dma((row_n - 1,)),
            dma((row_n - 1,)),
            dma((ITERS, col_n - 1)),
            dma((ITERS, col_n - 1)),
            dma((ITERS, row_n - 1)),
            dma((ITERS, row_n - 1)),
        ],
        compiler_params=pltpu.CompilerParams(
            collective_id=1, has_side_effects=True, vmem_limit_bytes=60 << 20
        ),
        cost_estimate=pl.CostEstimate(
            flops=12 * ns * nt * depth, bytes_accessed=2 * (ns + nt) * depth, transcendentals=2 * ns * nt
        ),
    )(source, target)
    return f.reshape(ns), g.reshape(nt)


def on_device(row_n, col_n, source, target):
    own_s, depth = source.shape
    own_t = target.shape[0]
    ns, nt = own_s * col_n, own_t * row_n
    vmem = pl.BlockSpec(memory_space=pltpu.VMEM)
    dma = pltpu.SemaphoreType.DMA
    f, g = pl.pallas_call(
        functools.partial(kernel, row_n, col_n),
        out_shape=(jax.ShapeDtypeStruct((1, ns), F32), jax.ShapeDtypeStruct((1, nt), F32)),
        in_specs=[vmem, vmem],
        out_specs=(vmem, vmem),
        scratch_shapes=[
            pltpu.VMEM((ns, depth), BF16),
            pltpu.VMEM((nt, depth), BF16),
            pltpu.VMEM((ns, depth), BF16),
            pltpu.VMEM((nt, depth), BF16),
            pltpu.VMEM((ns, nt), BF16),
            pltpu.VMEM((8, ns), F32),
            pltpu.VMEM((8, nt), F32),
            pltpu.VMEM((nt, depth), F32),
            pltpu.VMEM((ns, 128), F32),
            pltpu.VMEM((1, nt), F32),
            pltpu.VMEM((2 * ITERS, 1, max(ns, nt)), F32),
            pltpu.VMEM((2, 1, nt), F32),
            pltpu.VMEM((1, ns), F32),
            pltpu.VMEM((1, nt), F32),
            pltpu.VMEM((1, ns), F32),
            pltpu.VMEM((1, nt), F32),
            pltpu.VMEM((ITERS, col_n - 1, 1, ns), F32),
            pltpu.VMEM((ITERS, row_n - 1, 1, nt), F32),
            dma((col_n // 2,)),
            dma((col_n // 2,)),
            dma((row_n,)),
            dma((row_n,)),
            dma((col_n // 2,)),
            dma((col_n // 2,)),
            dma((ITERS, 2, col_n - 1)),
            dma((ITERS, 2, col_n - 1)),
            dma((ITERS, 2, row_n - 1)),
            dma((ITERS, 2, row_n - 1)),
        ],
        compiler_params=pltpu.CompilerParams(
            collective_id=0, has_side_effects=True, vmem_limit_bytes=60 << 20
        ),
        cost_estimate=pl.CostEstimate(
            flops=12 * ns * nt * depth, bytes_accessed=2 * (ns + nt) * depth, transcendentals=2 * ns * nt
        ),
    )(source, target)
    fast = f.reshape(ns), g.reshape(nt)
    return lax.cond(jnp.isnan(f[0, 0]), lambda: careful(row_n, col_n, source, target), lambda: fast)


def solution(mesh):
    placed = (P(("row", "col"), None), P(("col", "row"), None))
    return jax.shard_map(
        functools.partial(on_device, mesh.shape["row"], mesh.shape["col"]),
        mesh=mesh,
        in_specs=placed,
        out_specs=(P("row"), P("col")),
        check_vma=False,
    )
```

```python
import functools
import math

import jax
import jax.numpy as jnp
from jax import lax
from jax.experimental import pallas as pl
from jax.experimental.pallas import tpu as pltpu
from jax.sharding import PartitionSpec as P

ITERS = 3
EPS = 0.02
LOG2E = 1.0 / math.log(2.0)
SCALE = 2.0 * LOG2E / EPS
BACK = EPS / LOG2E
FLOOR = 90.0
CEIL = 100.0
F32 = jnp.float32
BF16 = jnp.bfloat16
MESH = pl.DeviceIdType.MESH


def log2(x):
    return jnp.log(x) * LOG2E


def split3(x):
    high = x.astype(BF16).astype(F32)
    mid = (x - high).astype(BF16).astype(F32)
    return high, mid, x - high - mid


def pick3(x, index, base, other):
    high, mid, low = split3(x)
    found = jnp.where(index == base + 1, mid, jnp.where(index == base + 2, low, other))
    return jnp.where(index == base, high, found).astype(BF16)


def nt_dot(x, y):
    return lax.dot_general(x, y, (((1,), (1,)), ((), ())), preferred_element_type=F32)


def kernel(
    row_n, col_n, s_ref, t_ref, f_ref, g_ref,
    s_all, t_all, s_ext, t_ext, kept, sums, sums_t, highs, row_part, col_part, part, weight, s_sq, t_sq, shift_s, shift_t, sample, g_first,
    from_col, from_row,
    s_send, s_recv, near_send, near_recv, far_send, far_recv, pair_send, pair_recv, col_send, col_recv, row_send, row_recv,
):
    own_s, depth = s_ref.shape
    own_t = t_ref.shape[0]
    ns, nt = own_s * col_n, own_t * row_n
    total_s, total_t = float(ns * row_n), float(nt * col_n)
    my_row, my_col = lax.axis_index("row"), lax.axis_index("col")
    col_peers = [lax.rem(my_col + k, col_n) for k in range(1, col_n)]
    row_peers = [lax.rem(my_row + k, row_n) for k in range(1, row_n)]
    my_core = lax.rem(my_col, 2)
    twin = my_col + 1 - 2 * my_core
    chips = col_n // 2

    barrier = pltpu.get_barrier_semaphore()
    for peer in col_peers:
        pl.semaphore_signal(barrier, inc=1, device_id={"col": peer}, device_id_type=MESH)
    for peer in row_peers:
        pl.semaphore_signal(barrier, inc=1, device_id={"row": peer}, device_id_type=MESH)

    def s_block(index):
        return pl.ds(pl.multiple_of(index * own_s, own_s), own_s)

    side = math.isqrt(row_n)
    my_z, my_x = my_row // side, my_row % side
    half_own = own_t // 2
    chunk_t = side * half_own
    chunks = 2 * side

    def first_halves(z, x):
        return pl.ds(pl.multiple_of((z * side + x) * half_own, half_own), half_own)

    def second_halves(z, x):
        return pl.ds(pl.multiple_of(nt // 2 + (x * side + z) * half_own, half_own), half_own)

    def steps(p):
        k = p // 2
        return k + k // 2 - 2 * (k // 3)

    def chunk_rows(p, sent=False):
        second = p % 2
        k = 0 if sent else steps(p)
        line = (my_z * (1 - second) + my_x * second - k + side) % side
        return pl.ds(pl.multiple_of(second * (nt // 2) + line * chunk_t, chunk_t), chunk_t)

    def s_from(k):
        return lax.rem(my_col - 2 * k + col_n, col_n)

    def twin_from(k):
        return lax.rem(twin - 2 * k + col_n, col_n)

    def near_copies():
        copies = []
        for k in range(1, side):
            for second in range(2):
                z = (my_z + k * second) % side
                x = (my_x + k * (1 - second)) % side
                here = t_ref.at[pl.ds(second * half_own, half_own), :]
                there = t_all.at[second_halves(my_z, my_x) if second else first_halves(my_z, my_x), :]
                copies.append(
                    pltpu.make_async_remote_copy(
                        here, there, near_send.at[second, k], near_recv.at[second, k],
                        device_id={"row": z * side + x}, device_id_type=MESH,
                    )
                )
        return copies

    def chunk_copy(p):
        second = p % 2
        at = t_all.at[chunk_rows(p, True), :]
        z = (my_z + steps(p) * (1 - second)) % side
        x = (my_x + steps(p) * second) % side
        return pltpu.make_async_remote_copy(
            at, at, far_send.at[p], far_recv.at[p], device_id={"row": z * side + x}, device_id_type=MESH
        )

    def s_copy(k):
        return pltpu.make_async_remote_copy(
            s_ref, s_all.at[s_block(my_col), :], s_send.at[k], s_recv.at[k],
            device_id={"col": lax.rem(my_col + 2 * k, col_n)}, device_id_type=MESH,
        )

    def twin_copy(k):
        at = s_all.at[s_block(s_from(k)), :]
        return pltpu.make_async_remote_copy(
            s_ref if k == 0 else at, at, pair_send.at[k], pair_recv.at[k], device_id={"col": twin}, device_id_type=MESH
        )

    pl.semaphore_wait(barrier, col_n + row_n - 2)
    for copy in near_copies():
        copy.start()
    for k in range(1, chips):
        s_copy(k).start()
    twin_copy(0).start()

    chunk = 128

    def ones_at(rows, first):
        lane = lax.broadcasted_iota(jnp.int32, (rows, depth), 1)
        return lane, jnp.where((lane >= first) & (lane < first + 3), 1.0, 0.0)

    def spread(column):
        return jnp.broadcast_to(column, (column.shape[0], depth))

    def along_lanes(ext, first):
        select = ones_at(16, first)[1].astype(BF16)
        return nt_dot(select, ext)[0:1, :]

    def bias_beside(x):
        x = x.astype(F32)
        lane, ones = ones_at(x.shape[0], 3)
        return pick3(spread(jnp.sum(x * x, axis=1, keepdims=True) * -0.5), lane, 0, ones)

    def t_prepare(p):
        t_ext[chunk_rows(p), :] = bias_beside(t_all[chunk_rows(p), :])

    def s_prepare(i):
        lane, ones = ones_at(own_s, 0)
        x = jnp.concatenate([s_all[s_block(i), :], ones.astype(BF16)], axis=1)
        shift = spread(-FLOOR / SCALE - jnp.max(nt_dot(x, sample[...]), axis=1, keepdims=True))
        s_ext[s_block(i), :] = pick3(shift, lane, 3, ones)

    s_all[s_block(my_col), :] = s_ref[...]
    t_all[first_halves(my_z, my_x), :] = t_ref[0:half_own, :]
    t_all[second_halves(my_z, my_x), :] = t_ref[half_own:own_t, :]
    sample[...] = jnp.concatenate([t_ref[...], bias_beside(t_ref[...])], axis=1)
    sums[...] = jnp.zeros_like(sums)
    highs[...] = jnp.full_like(highs, -3e38)
    s_prepare(my_col)
    for copy in near_copies():
        copy.wait()
    for p in range(2, chunks):
        chunk_copy(p).start()
    for p in range(2):
        t_prepare(p)

    half_s, half_t = ns // 2, nt // 2
    halves = (0, 1)

    def s_half(h):
        return pl.ds(h * half_s, half_s)

    def t_half(h):
        return pl.ds(h * half_t, half_t)

    def terms_with(p, h):
        x = jnp.concatenate([t_all[chunk_rows(p), :], t_ext[chunk_rows(p), :]], axis=1)
        high = highs[chunk_rows(p), :]
        for i in range(h * col_n // 2, (h + 1) * col_n // 2):
            at = pl.ds(i * own_s, own_s)
            z = nt_dot(x, jnp.concatenate([s_all[at, :], s_ext[at, :]], axis=1))
            for c in range(0, own_s, depth):
                high = jnp.maximum(high, z[:, c : c + depth])
            terms = jnp.exp2(z * SCALE).reshape(chunk_t // 8, 8, own_s)
            sums[:, at] = sums[:, at] + jnp.sum(terms, axis=0)
        highs[chunk_rows(p), :] = high

    def over(axis, turn, h):
        if axis == "col":
            here, there, send, recv, peers, at = part.at[2 * turn], from_col, col_send, col_recv, col_peers, s_half(h)
        else:
            here, there, send, recv, peers, at = part.at[2 * turn + 1], from_row, row_send, row_recv, row_peers, t_half(h)
        return [
            pltpu.make_async_remote_copy(
                here.at[:, at], there.at[turn, k, :, at], send.at[turn, h, k], recv.at[turn, h, k],
                device_id={axis: peer}, device_id_type=MESH,
            )
            for k, peer in enumerate(peers)
        ]

    def start(axis, turn, h):
        for copy in over(axis, turn, h):
            copy.start()

    def finish(axis, turn, h):
        for copy in over(axis, turn, h):
            copy.wait()
        if axis == "col":
            return [part[2 * turn, :, s_half(h)]] + [from_col[turn, k, :, s_half(h)] for k in range(col_n - 1)]
        return [part[2 * turn + 1, :, t_half(h)]] + [from_row[turn, k, :, t_half(h)] for k in range(row_n - 1)]

    def combined_logs(logs):
        highest = functools.reduce(jnp.maximum, logs)
        return highest + log2(sum(jnp.exp2(x - highest) for x in logs))

    def send_logs(h):
        at = s_half(h)
        shift_s[:, at] = along_lanes(s_ext[at, :], 3)
        found = jnp.sum(sums[:, at], axis=0, keepdims=True)
        logs = log2(found) - shift_s[:, at] * SCALE
        part[0, :, at] = jnp.where(found < 2.0**120, logs, jnp.nan)
        start("col", 0, h)

    for k in range(1, chips):
        s_copy(k).wait_recv()
        twin_copy(k).start()
        s_prepare(s_from(k))
    for k in range(chips):
        twin_copy(k).wait_recv()
        s_prepare(twin_from(k))

    def early(p, _):
        terms_with(p, 0)

        @pl.when((p > 0) & (p < chunks - 1))
        def _():
            chunk_copy(p + 1).wait_recv()
            t_prepare(p + 1)

        return 0

    def late(p, _):
        terms_with(p, 1)
        return 0

    lax.fori_loop(0, chunks, early, 0)
    send_logs(0)
    lax.fori_loop(0, chunks, late, 0)
    send_logs(1)

    for k in range(1, chips):
        s_copy(k).wait_send()
    for k in range(chips):
        twin_copy(k).wait_send()
    for p in range(2, chunks):
        chunk_copy(p).wait_send()

    room = (FLOOR + math.log2(total_t) - CEIL) / SCALE

    def t_shift(i, _):
        size = min(512, nt)
        lane, ones = ones_at(size, 0)
        rows = pl.ds(pl.multiple_of(i * size, size), size)
        bias = jnp.sum(jnp.where(lane < 3, t_ext[rows, :].astype(F32), 0.0), axis=1, keepdims=True)
        shift = spread(bias - jnp.max(highs[rows, :], axis=1, keepdims=True) - room)
        t_ext[rows, :] = pick3(shift, lane, 3, ones)
        return 0

    t_sq[...] = -2.0 * along_lanes(t_ext[...], 0)
    lax.fori_loop(0, nt // min(512, nt), t_shift, 0)
    shift_t[...] = along_lanes(t_ext[...], 3)

    width = min(512, half_t)

    def second(h):
        def one(i, _):
            at = pl.ds(pl.multiple_of(i * width, width), width)
            rows = s_half(h)
            x = jnp.concatenate([s_all[rows, :], s_ext[rows, :]], axis=1)
            w = jnp.concatenate([t_all[at, :], t_ext[at, :]], axis=1)
            terms = jnp.exp2(nt_dot(x, w) * SCALE)
            kept[rows, at] = terms.astype(BF16)
            summed = jnp.sum(terms.reshape(half_s // 8, 8, width), axis=0)
            if h == 0:
                sums_t[:, at] = summed
            else:
                summed = jnp.sum(summed + sums_t[:, at], axis=0, keepdims=True)
                part[1, :, at] = log2(summed) - shift_t[:, at] * SCALE
            return 0

        return one

    for h in halves:
        at = s_half(h)
        f_ref[:, at] = math.log2(total_t) - combined_logs(finish("col", 0, h))

        def s_bias(i, _):
            size = min(512, half_s)
            lane, ones = ones_at(size, 3)
            rows = pl.ds(pl.multiple_of(i * size + h * half_s, size), size)
            bias = jnp.transpose(jnp.broadcast_to(f_ref[:, rows] * (1.0 / SCALE), (depth, size)))
            s_ext[rows, :] = pick3(bias, lane, 0, ones)
            return 0

        lax.fori_loop(0, half_s // min(512, half_s), s_bias, 0)
        if h == 0:
            lax.fori_loop(0, nt // width, second(h), 0)
    for h in halves:
        lax.fori_loop(h * half_t // width, (h + 1) * half_t // width, second(1), 0)
        start("row", 0, h)

    def s_norms(i, _):
        ones = jnp.full((16, depth), 1.0, BF16)
        rows = pl.ds(pl.multiple_of(i * own_s, own_s), own_s)
        x = s_all[rows, :].astype(F32)
        square = x * x
        high = square.astype(BF16)
        low = (square - high.astype(F32)).astype(BF16)
        s_sq[:, rows] = (nt_dot(ones, high) + nt_dot(ones, low))[0:1, :]
        return 0

    lax.fori_loop(0, col_n, s_norms, 0)

    size = min(512, half_s)
    fine = min(64, size)

    def row_sums(h, out):
        def one(i, _):
            for q in range(0, size, 128):
                pieces = []
                for r in range(q, q + 128, fine):
                    rows = pl.ds(pl.multiple_of(i * size, size) + r, fine)
                    summed = jnp.zeros((fine, 128), F32) if out is None else row_part[rows, :]
                    for c in range(h * half_t, (h + 1) * half_t, 128):
                        summed = summed + kept[rows, c : c + 128].astype(F32) * weight[1, :, c : c + 128]
                    if out is None:
                        row_part[rows, :] = summed
                    pieces.append(summed)
                if out is not None:
                    turned = jnp.transpose(jnp.concatenate(pieces, axis=0))
                    at = pl.ds(pl.multiple_of(i * size, size) + q, 128)
                    out[:, at] = jnp.sum(turned, axis=0, keepdims=True)
            return 0

        return one

    def col_sums(lhs, h, at):
        got = jnp.dot(lhs, kept[s_half(h), at], preferred_element_type=F32)
        return jnp.sum(got, axis=0, keepdims=True)

    def lhs_of(x):
        index = lax.broadcasted_iota(jnp.int32, (16, half_s), 0)
        return pick3(jnp.broadcast_to(x, (16, half_s)), index, 0, 0.0)

    for turn in range(1, ITERS + 1):
        for h in halves:
            at = t_half(h)
            arrived = finish("row", turn - 1, h)
            if turn == 1:
                logs = combined_logs(arrived)
                held = logs + shift_t[:, at] * SCALE
                g_first[:, at] = jnp.where(held > -30.0, math.log2(total_s) - logs, jnp.nan)
                weight[0, :, at] = jnp.exp2(g_first[:, at] - shift_t[:, at] * SCALE)
                weight[1, :, at] = weight[0, :, at]
            else:
                v = total_s / sum(arrived)
                if turn < ITERS:
                    weight[1, :, at] = weight[0, :, at] * v
                else:
                    found = BACK * (g_first[:, at] + log2(v)) + t_sq[:, at]
                    for i in range(row_n):
                        z, x = (i % side, i // side) if h else (i // side, i % side)
                        begin = (z * side + x) * own_t + h * half_own
                        g_ref[:, begin : begin + half_own] = found[:, i * half_own : (i + 1) * half_own]
            if turn < ITERS and h == 0:
                lax.fori_loop(0, ns // size, row_sums(0, None), 0)
        if turn == ITERS:
            break
        for h in halves:
            lax.fori_loop(h * half_s // size, (h + 1) * half_s // size, row_sums(1, part.at[2 * turn]), 0)
            start("col", turn, h)
        for h in halves:
            u = total_t / sum(finish("col", turn, h))
            if turn == ITERS - 1:
                f_ref[:, s_half(h)] = BACK * (f_ref[:, s_half(h)] + log2(u)) + s_sq[:, s_half(h)]
            lhs = lhs_of(u)
            for c in halves:
                at = t_half(c)
                got = col_sums(lhs, h, at)
                if h == 0:
                    col_part[:, at] = got
                else:
                    part[2 * turn + 1, :, at] = (got + col_part[:, at]) * weight[0, :, at]
                    start("row", turn, c)


def careful_kernel(
    row_n, col_n, s_ref, t_ref, f_ref, g_ref,
    s_all, t_all, s_ext, t_ext, kept, z0, z1, part, col_high, s_sq, t_sq, from_col, from_row,
    s_send, s_recv, t_send, t_recv, col_send, col_recv, row_send, row_recv,
):
    own_s, depth = s_ref.shape
    own_t = t_ref.shape[0]
    ns, nt = own_s * col_n, own_t * row_n
    total_s, total_t = float(ns * row_n), float(nt * col_n)
    my_row, my_col = lax.axis_index("row"), lax.axis_index("col")
    col_peers = [lax.rem(my_col + k, col_n) for k in range(1, col_n)]
    row_peers = [lax.rem(my_row + k, row_n) for k in range(1, row_n)]

    barrier = pltpu.get_barrier_semaphore()
    for peer in col_peers:
        pl.semaphore_signal(barrier, inc=1, device_id={"col": peer}, device_id_type=MESH)
    for peer in row_peers:
        pl.semaphore_signal(barrier, inc=1, device_id={"row": peer}, device_id_type=MESH)
    pl.semaphore_wait(barrier, col_n + row_n - 2)

    s_rows = pl.ds(pl.multiple_of(my_col * own_s, own_s), own_s)
    t_rows = pl.ds(pl.multiple_of(my_row * own_t, own_t), own_t)
    gathers = []
    for k, peer in enumerate(row_peers):
        gathers.append(
            pltpu.make_async_remote_copy(
                t_ref, t_all.at[t_rows, :], t_send.at[k], t_recv.at[k],
                device_id={"row": peer}, device_id_type=MESH,
            )
        )
    for k, peer in enumerate(col_peers):
        gathers.append(
            pltpu.make_async_remote_copy(
                s_ref, s_all.at[s_rows, :], s_send.at[k], s_recv.at[k],
                device_id={"col": peer}, device_id_type=MESH,
            )
        )
    for copy in gathers:
        copy.start()
    s_all[s_rows, :] = s_ref[...]
    t_all[t_rows, :] = t_ref[...]
    for copy in gathers:
        copy.wait()

    chunk = min(512, own_s, own_t)
    lane = lax.broadcasted_iota(jnp.int32, (chunk, depth), 1)
    ones = jnp.where(lane < 3, 1.0, 0.0).astype(BF16)

    def s_prepare(i, _):
        rows = pl.ds(pl.multiple_of(i * chunk, chunk), chunk)
        x = s_all[rows, :].astype(F32)
        s_sq[:, rows] = jnp.sum(jnp.transpose(x * x), axis=0, keepdims=True)
        s_ext[rows, :] = ones
        return 0

    def t_prepare(i, _):
        rows = pl.ds(pl.multiple_of(i * chunk, chunk), chunk)
        x = t_all[rows, :].astype(F32)
        t_sq[:, rows] = jnp.sum(jnp.transpose(x * x), axis=0, keepdims=True)
        bias = jnp.sum(x * x, axis=1, keepdims=True) * -0.5
        t_ext[rows, :] = pick3(jnp.broadcast_to(bias, (chunk, depth)), lane, 0, 0.0)
        return 0

    lax.fori_loop(0, ns // chunk, s_prepare, 0)
    lax.fori_loop(0, nt // chunk, t_prepare, 0)

    def logs_pass(x_all, x_ext, w_all, w_ext, out, keep):
        nx, nw = x_all.shape[0], w_all.shape[0]
        width = z0.shape[1]
        tiles = nw // width
        step = min(512, nx)
        fine = min(64, step)

        def lanes(tile):
            return pl.ds(pl.multiple_of(tile * width, width), width)

        def scores(tile, q, z, highest):
            rows = pl.ds(q * step, step)
            at = lanes(tile)
            x = jnp.concatenate([x_all[rows, :], x_ext[rows, :]], axis=1)
            w = jnp.concatenate([w_all[at, :], w_ext[at, :]], axis=1)
            inner = nt_dot(x, w)
            z[rows, :] = inner
            return jnp.maximum(highest, jnp.max(inner.reshape(step // 8, 8, width), axis=0))

        def sums(tile, q, z, highest, summed):
            for j in range(q * step, (q + 1) * step, fine):
                rows = pl.ds(j, fine)
                shifted = z[rows, :].reshape(fine // 8, 8, width) - highest[None]
                terms = jnp.exp2(shifted * SCALE)
                if keep:
                    kept[rows, lanes(tile)] = terms.reshape(fine, width).astype(BF16)
                summed = summed + jnp.sum(terms, axis=0)
            return summed

        def settle(highest):
            return jnp.broadcast_to(jnp.max(highest, axis=0, keepdims=True), (8, width))

        low = jnp.full((8, width), -3e38, F32)

        def both(tile, z_now, highest, z_next):
            following = jnp.minimum(tile + 1, tiles - 1)
            new_high = low
            summed = jnp.zeros((8, width), F32)
            for q in range(nx // step):
                new_high = scores(following, q, z_next, new_high)
                summed = sums(tile, q, z_now, highest, summed)
            top = highest[0:1, :] * SCALE
            out[:, lanes(tile)] = top + log2(jnp.sum(summed, axis=0, keepdims=True))
            if keep:
                col_high[:, lanes(tile)] = top
            return settle(new_high)

        def pair(i, highest):
            highest = both(2 * i, z0, highest, z1)
            return both(2 * i + 1, z1, highest, z0)

        first = low
        for q in range(nx // step):
            first = scores(0, q, z0, first)
        lax.fori_loop(0, tiles // 2, pair, settle(first))

    def exchange(turn, sent, received, send, recv, axis, peers):
        copies = [
            pltpu.make_async_remote_copy(
                sent, received.at[turn, k], send.at[turn, k], recv.at[turn, k],
                device_id={axis: peer}, device_id_type=MESH,
            )
            for k, peer in enumerate(peers)
        ]
        for copy in copies:
            copy.start()
        for copy in copies:
            copy.wait()
        return [sent[...]] + [received[turn, k] for k in range(len(peers))]

    def over_col(turn):
        return exchange(turn, part.at[2 * turn], from_col, col_send, col_recv, "col", col_peers)

    def over_row(turn):
        return exchange(turn, part.at[2 * turn + 1], from_row, row_send, row_recv, "row", row_peers)

    def combined_logs(logs):
        highest = functools.reduce(jnp.maximum, logs)
        return highest + log2(sum(jnp.exp2(x - highest) for x in logs))

    logs_pass(t_all, t_ext, s_all, s_ext, part.at[0], False)
    f_first = math.log2(total_t) - combined_logs(over_col(0))
    f_ref[...] = f_first

    def s_bias(i, _):
        rows = pl.ds(pl.multiple_of(i * chunk, chunk), chunk)
        bias = jnp.transpose(jnp.broadcast_to(f_ref[:, rows] * (1.0 / SCALE), (depth, chunk)))
        s_ext[rows, :] = pick3(bias, lane, 0, 0.0)
        return 0

    def t_ones(i, _):
        t_ext[pl.ds(pl.multiple_of(i * chunk, chunk), chunk), :] = ones
        return 0

    lax.fori_loop(0, ns // chunk, s_bias, 0)
    lax.fori_loop(0, nt // chunk, t_ones, 0)
    logs_pass(s_all, s_ext, t_all, t_ext, part.at[1], True)
    g_first = math.log2(total_s) - combined_logs(over_row(0))
    g_ref[...] = g_first
    col_high[...] = jnp.exp2(g_first + col_high[...])

    block = min(512, ns, nt)

    def parts_of(x):
        index = lax.broadcasted_iota(jnp.int32, (16, x.shape[1]), 0)
        return pick3(jnp.broadcast_to(x, (16, x.shape[1])), index, 0, 0.0)

    def row_sums(x, out):
        lhs = parts_of(x)

        def one(i, _):
            rows = pl.ds(pl.multiple_of(i * block, block), block)
            out[:, rows] = jnp.sum(nt_dot(lhs, kept[rows, :]), axis=0, keepdims=True)
            return 0

        lax.fori_loop(0, ns // block, one, 0)

    def col_sums(x, out):
        lhs = parts_of(x)

        def one(i, _):
            at = pl.ds(pl.multiple_of(i * block, block), block)
            found = jnp.dot(lhs, kept[:, at], preferred_element_type=F32)
            out[:, at] = jnp.sum(found, axis=0, keepdims=True) * col_high[:, at]
            return 0

        lax.fori_loop(0, nt // block, one, 0)

    weight = col_high[...]
    for turn in range(1, ITERS):
        row_sums(weight, part.at[2 * turn])
        u = total_t / sum(over_col(turn))
        col_sums(u, part.at[2 * turn + 1])
        v = total_s / sum(over_row(turn))
        weight = col_high[...] * v
    f_ref[...] = BACK * (f_ref[...] + log2(u)) + s_sq[...]
    g_ref[...] = BACK * (g_ref[...] + log2(v)) + t_sq[...]


def careful(row_n, col_n, source, target):
    own_s, depth = source.shape
    own_t = target.shape[0]
    ns, nt = own_s * col_n, own_t * row_n
    width = min(256, ns // 2, nt // 2)
    vmem = pl.BlockSpec(memory_space=pltpu.VMEM)
    dma = pltpu.SemaphoreType.DMA
    f, g = pl.pallas_call(
        functools.partial(careful_kernel, row_n, col_n),
        out_shape=(jax.ShapeDtypeStruct((1, ns), F32), jax.ShapeDtypeStruct((1, nt), F32)),
        in_specs=[vmem, vmem],
        out_specs=(vmem, vmem),
        scratch_shapes=[
            pltpu.VMEM((ns, depth), BF16),
            pltpu.VMEM((nt, depth), BF16),
            pltpu.VMEM((ns, depth), BF16),
            pltpu.VMEM((nt, depth), BF16),
            pltpu.VMEM((ns, nt), BF16),
            pltpu.VMEM((max(ns, nt), width), F32),
            pltpu.VMEM((max(ns, nt), width), F32),
            pltpu.VMEM((2 * ITERS, 1, max(ns, nt)), F32),
            pltpu.VMEM((1, nt), F32),
            pltpu.VMEM((1, ns), F32),
            pltpu.VMEM((1, nt), F32),
            pltpu.VMEM((ITERS, col_n - 1, 1, ns), F32),
            pltpu.VMEM((ITERS, row_n - 1, 1, nt), F32),
            dma((col_n - 1,)),
            dma((col_n - 1,)),
            dma((row_n - 1,)),
            dma((row_n - 1,)),
            dma((ITERS, col_n - 1)),
            dma((ITERS, col_n - 1)),
            dma((ITERS, row_n - 1)),
            dma((ITERS, row_n - 1)),
        ],
        compiler_params=pltpu.CompilerParams(
            collective_id=1, has_side_effects=True, vmem_limit_bytes=60 << 20
        ),
        cost_estimate=pl.CostEstimate(
            flops=12 * ns * nt * depth, bytes_accessed=2 * (ns + nt) * depth, transcendentals=2 * ns * nt
        ),
    )(source, target)
    return f.reshape(ns), g.reshape(nt)


def on_device(row_n, col_n, source, target):
    own_s, depth = source.shape
    own_t = target.shape[0]
    ns, nt = own_s * col_n, own_t * row_n
    vmem = pl.BlockSpec(memory_space=pltpu.VMEM)
    dma = pltpu.SemaphoreType.DMA
    f, g = pl.pallas_call(
        functools.partial(kernel, row_n, col_n),
        out_shape=(jax.ShapeDtypeStruct((1, ns), F32), jax.ShapeDtypeStruct((1, nt), F32)),
        in_specs=[vmem, vmem],
        out_specs=(vmem, vmem),
        scratch_shapes=[
            pltpu.VMEM((ns, depth), BF16),
            pltpu.VMEM((nt, depth), BF16),
            pltpu.VMEM((ns, depth), BF16),
            pltpu.VMEM((nt, depth), BF16),
            pltpu.VMEM((ns, nt), BF16),
            pltpu.VMEM((8, ns), F32),
            pltpu.VMEM((8, nt), F32),
            pltpu.VMEM((nt, depth), F32),
            pltpu.VMEM((ns, 128), F32),
            pltpu.VMEM((1, nt), F32),
            pltpu.VMEM((2 * ITERS, 1, max(ns, nt)), F32),
            pltpu.VMEM((2, 1, nt), F32),
            pltpu.VMEM((1, ns), F32),
            pltpu.VMEM((1, nt), F32),
            pltpu.VMEM((1, ns), F32),
            pltpu.VMEM((1, nt), F32),
            pltpu.VMEM((own_t, 2 * depth), BF16),
            pltpu.VMEM((1, nt), F32),
            pltpu.VMEM((ITERS, col_n - 1, 1, ns), F32),
            pltpu.VMEM((ITERS, row_n - 1, 1, nt), F32),
            dma((col_n // 2,)),
            dma((col_n // 2,)),
            dma((2, math.isqrt(row_n))),
            dma((2, math.isqrt(row_n))),
            dma((2 * math.isqrt(row_n),)),
            dma((2 * math.isqrt(row_n),)),
            dma((col_n // 2,)),
            dma((col_n // 2,)),
            dma((ITERS, 2, col_n - 1)),
            dma((ITERS, 2, col_n - 1)),
            dma((ITERS, 2, row_n - 1)),
            dma((ITERS, 2, row_n - 1)),
        ],
        compiler_params=pltpu.CompilerParams(
            collective_id=0, has_side_effects=True, vmem_limit_bytes=60 << 20
        ),
        cost_estimate=pl.CostEstimate(
            flops=12 * ns * nt * depth, bytes_accessed=2 * (ns + nt) * depth, transcendentals=2 * ns * nt
        ),
    )(source, target)
    fast = f.reshape(ns), g.reshape(nt)
    return lax.cond(jnp.isnan(f[0, 0]), lambda: careful(row_n, col_n, source, target), lambda: fast)


def solution(mesh):
    placed = (P(("row", "col"), None), P(("col", "row"), None))
    return jax.shard_map(
        functools.partial(on_device, mesh.shape["row"], mesh.shape["col"]),
        mesh=mesh,
        in_specs=placed,
        out_specs=(P("row"), P("col")),
        check_vma=False,
    )
```

```python
import functools
import math

import jax
import jax.numpy as jnp
from jax import lax
from jax.experimental import pallas as pl
from jax.experimental.pallas import tpu as pltpu
from jax.sharding import PartitionSpec as P

ITERS = 3
EPS = 0.02
LOG2E = 1.0 / math.log(2.0)
SCALE = 2.0 * LOG2E / EPS
BACK = EPS / LOG2E
FLOOR = 90.0
CEIL = 100.0
F32 = jnp.float32
BF16 = jnp.bfloat16
MESH = pl.DeviceIdType.MESH


def log2(x):
    return jnp.log(x) * LOG2E


def split3(x):
    high = x.astype(BF16).astype(F32)
    mid = (x - high).astype(BF16).astype(F32)
    return high, mid, x - high - mid


def pick3(x, index, base, other):
    high, mid, low = split3(x)
    found = jnp.where(index == base + 1, mid, jnp.where(index == base + 2, low, other))
    return jnp.where(index == base, high, found).astype(BF16)


def nt_dot(x, y):
    return lax.dot_general(x, y, (((1,), (1,)), ((), ())), preferred_element_type=F32)


def kernel(
    row_n, col_n, s_ref, t_ref, f_ref, g_ref,
    s_all, t_all, s_ext, t_ext, kept, sums, sums_t, highs, row_part, col_part, part, weight, s_sq, t_sq, shift_s, shift_t, sample, g_first, weight_low,
    from_col, from_row,
    s_send, s_recv, near_send, near_recv, far_send, far_recv, pair_send, pair_recv, col_send, col_recv, row_send, row_recv,
):
    own_s, depth = s_ref.shape
    own_t = t_ref.shape[0]
    ns, nt = own_s * col_n, own_t * row_n
    total_s, total_t = float(ns * row_n), float(nt * col_n)
    my_row, my_col = lax.axis_index("row"), lax.axis_index("col")
    col_peers = [lax.rem(my_col + k, col_n) for k in range(1, col_n)]
    row_peers = [lax.rem(my_row + k, row_n) for k in range(1, row_n)]
    my_core = lax.rem(my_col, 2)
    twin = my_col + 1 - 2 * my_core
    chips = col_n // 2

    barrier = pltpu.get_barrier_semaphore()
    for peer in col_peers:
        pl.semaphore_signal(barrier, inc=1, device_id={"col": peer}, device_id_type=MESH)
    for peer in row_peers:
        pl.semaphore_signal(barrier, inc=1, device_id={"row": peer}, device_id_type=MESH)

    def s_block(index):
        return pl.ds(pl.multiple_of(index * own_s, own_s), own_s)

    side = math.isqrt(row_n)
    my_z, my_x = my_row // side, my_row % side
    half_own = own_t // 2
    chunk_t = side * half_own
    chunks = 2 * side

    def first_halves(z, x):
        return pl.ds(pl.multiple_of((z * side + x) * half_own, half_own), half_own)

    def second_halves(z, x):
        return pl.ds(pl.multiple_of(nt // 2 + (x * side + z) * half_own, half_own), half_own)

    def steps(p):
        k = p // 2
        return k + k // 2 - 2 * (k // 3)

    def chunk_rows(p, sent=False):
        second = p % 2
        k = 0 if sent else steps(p)
        line = (my_z * (1 - second) + my_x * second - k + side) % side
        return pl.ds(pl.multiple_of(second * (nt // 2) + line * chunk_t, chunk_t), chunk_t)

    def s_from(k):
        return lax.rem(my_col - 2 * k + col_n, col_n)

    def twin_from(k):
        return lax.rem(twin - 2 * k + col_n, col_n)

    def near_copies():
        copies = []
        for k in range(1, side):
            for second in range(2):
                z = (my_z + k * second) % side
                x = (my_x + k * (1 - second)) % side
                here = t_ref.at[pl.ds(second * half_own, half_own), :]
                there = t_all.at[second_halves(my_z, my_x) if second else first_halves(my_z, my_x), :]
                copies.append(
                    pltpu.make_async_remote_copy(
                        here, there, near_send.at[second, k], near_recv.at[second, k],
                        device_id={"row": z * side + x}, device_id_type=MESH,
                    )
                )
        return copies

    def chunk_copy(p):
        second = p % 2
        at = t_all.at[chunk_rows(p, True), :]
        z = (my_z + steps(p) * (1 - second)) % side
        x = (my_x + steps(p) * second) % side
        return pltpu.make_async_remote_copy(
            at, at, far_send.at[p], far_recv.at[p], device_id={"row": z * side + x}, device_id_type=MESH
        )

    def s_copy(k):
        return pltpu.make_async_remote_copy(
            s_ref, s_all.at[s_block(my_col), :], s_send.at[k], s_recv.at[k],
            device_id={"col": lax.rem(my_col + 2 * k, col_n)}, device_id_type=MESH,
        )

    def twin_copy(k):
        at = s_all.at[s_block(s_from(k)), :]
        return pltpu.make_async_remote_copy(
            s_ref if k == 0 else at, at, pair_send.at[k], pair_recv.at[k], device_id={"col": twin}, device_id_type=MESH
        )

    pl.semaphore_wait(barrier, col_n + row_n - 2)
    for copy in near_copies():
        copy.start()
    for k in range(1, chips):
        s_copy(k).start()
    twin_copy(0).start()

    chunk = 128

    def ones_at(rows, first):
        lane = lax.broadcasted_iota(jnp.int32, (rows, depth), 1)
        return lane, jnp.where((lane >= first) & (lane < first + 3), 1.0, 0.0)

    def spread(column):
        return jnp.broadcast_to(column, (column.shape[0], depth))

    def along_lanes(ext, first):
        select = ones_at(16, first)[1].astype(BF16)
        return nt_dot(select, ext)[0:1, :]

    def bias_beside(x):
        x = x.astype(F32)
        lane, ones = ones_at(x.shape[0], 3)
        return pick3(spread(jnp.sum(x * x, axis=1, keepdims=True) * -0.5), lane, 0, ones)

    def t_prepare(p):
        t_ext[chunk_rows(p), :] = bias_beside(t_all[chunk_rows(p), :])

    def s_prepare(i):
        lane, ones = ones_at(own_s, 0)
        x = jnp.concatenate([s_all[s_block(i), :], ones.astype(BF16)], axis=1)
        shift = spread(-FLOOR / SCALE - jnp.max(nt_dot(x, sample[...]), axis=1, keepdims=True))
        s_ext[s_block(i), :] = pick3(shift, lane, 3, ones)

    s_all[s_block(my_col), :] = s_ref[...]
    t_all[first_halves(my_z, my_x), :] = t_ref[0:half_own, :]
    t_all[second_halves(my_z, my_x), :] = t_ref[half_own:own_t, :]
    sample[...] = jnp.concatenate([t_ref[...], bias_beside(t_ref[...])], axis=1)
    sums[...] = jnp.zeros_like(sums)
    highs[...] = jnp.full_like(highs, -3e38)
    s_prepare(my_col)
    for copy in near_copies():
        copy.wait()
    for p in range(2, chunks):
        chunk_copy(p).start()
    for p in range(2):
        t_prepare(p)

    half_s, half_t = ns // 2, nt // 2
    halves = (0, 1)

    def s_half(h):
        return pl.ds(h * half_s, half_s)

    def t_half(h):
        return pl.ds(h * half_t, half_t)

    def terms_with(p, h):
        x = jnp.concatenate([t_all[chunk_rows(p), :], t_ext[chunk_rows(p), :]], axis=1)
        high = highs[chunk_rows(p), :]
        for i in range(h * col_n // 2, (h + 1) * col_n // 2):
            at = pl.ds(i * own_s, own_s)
            z = nt_dot(x, jnp.concatenate([s_all[at, :], s_ext[at, :]], axis=1))
            for c in range(0, own_s, depth):
                high = jnp.maximum(high, z[:, c : c + depth])
            terms = jnp.exp2(z * SCALE).reshape(chunk_t // 8, 8, own_s)
            sums[:, at] = sums[:, at] + jnp.sum(terms, axis=0)
        highs[chunk_rows(p), :] = high

    def over(axis, turn, h):
        if axis == "col":
            here, there, send, recv, peers, at = part.at[2 * turn], from_col, col_send, col_recv, col_peers, s_half(h)
        else:
            here, there, send, recv, peers, at = part.at[2 * turn + 1], from_row, row_send, row_recv, row_peers, t_half(h)
        return [
            pltpu.make_async_remote_copy(
                here.at[:, at], there.at[turn, k, :, at], send.at[turn, h, k], recv.at[turn, h, k],
                device_id={axis: peer}, device_id_type=MESH,
            )
            for k, peer in enumerate(peers)
        ]

    def start(axis, turn, h):
        for copy in over(axis, turn, h):
            copy.start()

    def finish(axis, turn, h):
        for copy in over(axis, turn, h):
            copy.wait()
        if axis == "col":
            return [part[2 * turn, :, s_half(h)]] + [from_col[turn, k, :, s_half(h)] for k in range(col_n - 1)]
        return [part[2 * turn + 1, :, t_half(h)]] + [from_row[turn, k, :, t_half(h)] for k in range(row_n - 1)]

    def combined_logs(logs):
        highest = functools.reduce(jnp.maximum, logs)
        return highest + log2(sum(jnp.exp2(x - highest) for x in logs))

    def send_logs(h):
        at = s_half(h)
        shift_s[:, at] = along_lanes(s_ext[at, :], 3)
        found = jnp.sum(sums[:, at], axis=0, keepdims=True)
        logs = log2(found) - shift_s[:, at] * SCALE
        part[0, :, at] = jnp.where(found < 2.0**120, logs, jnp.nan)
        start("col", 0, h)

    for k in range(1, chips):
        s_copy(k).wait_recv()
        twin_copy(k).start()
        s_prepare(s_from(k))
    for k in range(chips):
        twin_copy(k).wait_recv()
        s_prepare(twin_from(k))

    def early(p, _):
        terms_with(p, 0)

        @pl.when((p > 0) & (p < chunks - 1))
        def _():
            chunk_copy(p + 1).wait_recv()
            t_prepare(p + 1)

        return 0

    def late(p, _):
        terms_with(p, 1)
        return 0

    lax.fori_loop(0, chunks, early, 0)
    send_logs(0)
    lax.fori_loop(0, chunks, late, 0)
    send_logs(1)

    for k in range(1, chips):
        s_copy(k).wait_send()
    for k in range(chips):
        twin_copy(k).wait_send()
    for p in range(2, chunks):
        chunk_copy(p).wait_send()

    room = (FLOOR + math.log2(total_t) - CEIL) / SCALE

    def t_shift(i, _):
        size = min(512, nt)
        lane, ones = ones_at(size, 0)
        rows = pl.ds(pl.multiple_of(i * size, size), size)
        bias = jnp.sum(jnp.where(lane < 3, t_ext[rows, :].astype(F32), 0.0), axis=1, keepdims=True)
        shift = spread(bias - jnp.max(highs[rows, :], axis=1, keepdims=True) - room)
        t_ext[rows, :] = pick3(shift, lane, 3, ones)
        return 0

    t_sq[...] = -2.0 * along_lanes(t_ext[...], 0)
    lax.fori_loop(0, nt // min(512, nt), t_shift, 0)
    shift_t[...] = along_lanes(t_ext[...], 3)

    width = min(512, half_t)

    def second(h):
        def one(i, _):
            at = pl.ds(pl.multiple_of(i * width, width), width)
            rows = s_half(h)
            x = jnp.concatenate([s_all[rows, :], s_ext[rows, :]], axis=1)
            w = jnp.concatenate([t_all[at, :], t_ext[at, :]], axis=1)
            terms = jnp.exp2(nt_dot(x, w) * SCALE)
            kept[rows, at] = terms.astype(BF16)
            summed = jnp.sum(terms.reshape(half_s // 8, 8, width), axis=0)
            if h == 0:
                sums_t[:, at] = summed
            else:
                summed = jnp.sum(summed + sums_t[:, at], axis=0, keepdims=True)
                part[1, :, at] = log2(summed) - shift_t[:, at] * SCALE
            return 0

        return one

    for h in halves:
        at = s_half(h)
        f_ref[:, at] = math.log2(total_t) - combined_logs(finish("col", 0, h))

        def s_bias(i, _):
            size = min(512, half_s)
            lane, ones = ones_at(size, 3)
            rows = pl.ds(pl.multiple_of(i * size + h * half_s, size), size)
            bias = jnp.transpose(jnp.broadcast_to(f_ref[:, rows] * (1.0 / SCALE), (depth, size)))
            s_ext[rows, :] = pick3(bias, lane, 0, ones)
            return 0

        lax.fori_loop(0, half_s // min(512, half_s), s_bias, 0)
        if h == 0:
            lax.fori_loop(0, nt // width, second(h), 0)
    for h in halves:
        lax.fori_loop(h * half_t // width, (h + 1) * half_t // width, second(1), 0)
        start("row", 0, h)

    def s_norms(i, _):
        ones = jnp.full((16, depth), 1.0, BF16)
        rows = pl.ds(pl.multiple_of(i * own_s, own_s), own_s)
        x = s_all[rows, :].astype(F32)
        square = x * x
        high = square.astype(BF16)
        low = (square - high.astype(F32)).astype(BF16)
        s_sq[:, rows] = (nt_dot(ones, high) + nt_dot(ones, low))[0:1, :]
        return 0

    lax.fori_loop(0, col_n, s_norms, 0)

    size = min(512, half_s)
    fine = min(64, size)

    def set_weight(at, x):
        weight_low[:, at] = jnp.broadcast_to(x, (16, half_t)).astype(BF16)

    def row_sums(h, out):
        def one(i, _):
            for q in range(0, size, 128):
                pieces = []
                for r in range(q, q + 128, fine):
                    rows = pl.ds(pl.multiple_of(i * size, size) + r, fine)
                    summed = jnp.zeros((fine, 128), F32) if out is None else row_part[rows, :]
                    for c in range(h * half_t, (h + 1) * half_t, 512):
                        terms = [
                            kept[rows, d : d + 128] * jnp.tile(weight_low[:, d : d + 128], (fine // 16, 1))
                            for d in range(c, c + 512, 128)
                            if d < (h + 1) * half_t
                        ]
                        summed = summed + functools.reduce(jnp.add, terms).astype(F32)
                    if out is None:
                        row_part[rows, :] = summed
                    pieces.append(summed)
                if out is not None:
                    turned = jnp.transpose(jnp.concatenate(pieces, axis=0))
                    at = pl.ds(pl.multiple_of(i * size, size) + q, 128)
                    out[:, at] = jnp.sum(turned, axis=0, keepdims=True)
            return 0

        return one

    def col_sums(lhs, h, at):
        got = jnp.dot(lhs, kept[s_half(h), at], preferred_element_type=F32)
        return jnp.sum(got, axis=0, keepdims=True)

    def lhs_of(x):
        index = lax.broadcasted_iota(jnp.int32, (16, half_s), 0)
        return pick3(jnp.broadcast_to(x, (16, half_s)), index, 0, 0.0)

    for turn in range(1, ITERS + 1):
        for h in halves:
            at = t_half(h)
            arrived = finish("row", turn - 1, h)
            if turn == 1:
                logs = combined_logs(arrived)
                held = logs + shift_t[:, at] * SCALE
                g_first[:, at] = jnp.where(held > -30.0, math.log2(total_s) - logs, jnp.nan)
                weight[0, :, at] = jnp.exp2(g_first[:, at] - shift_t[:, at] * SCALE)
                set_weight(at, weight[0, :, at])
            else:
                v = total_s / sum(arrived)
                if turn < ITERS:
                    set_weight(at, weight[0, :, at] * v)
                else:
                    found = BACK * (g_first[:, at] + log2(v)) + t_sq[:, at]
                    for i in range(row_n):
                        z, x = (i % side, i // side) if h else (i // side, i % side)
                        begin = (z * side + x) * own_t + h * half_own
                        g_ref[:, begin : begin + half_own] = found[:, i * half_own : (i + 1) * half_own]
            if turn < ITERS and h == 0:
                lax.fori_loop(0, ns // size, row_sums(0, None), 0)
        if turn == ITERS:
            break
        for h in halves:
            lax.fori_loop(h * half_s // size, (h + 1) * half_s // size, row_sums(1, part.at[2 * turn]), 0)
            start("col", turn, h)
        for h in halves:
            u = total_t / sum(finish("col", turn, h))
            if turn == ITERS - 1:
                f_ref[:, s_half(h)] = BACK * (f_ref[:, s_half(h)] + log2(u)) + s_sq[:, s_half(h)]
            lhs = lhs_of(u)
            for c in halves:
                at = t_half(c)
                got = col_sums(lhs, h, at)
                if h == 0:
                    col_part[:, at] = got
                else:
                    part[2 * turn + 1, :, at] = (got + col_part[:, at]) * weight[0, :, at]
                    start("row", turn, c)


def careful_kernel(
    row_n, col_n, s_ref, t_ref, f_ref, g_ref,
    s_all, t_all, s_ext, t_ext, kept, z0, z1, part, col_high, s_sq, t_sq, from_col, from_row,
    s_send, s_recv, t_send, t_recv, col_send, col_recv, row_send, row_recv,
):
    own_s, depth = s_ref.shape
    own_t = t_ref.shape[0]
    ns, nt = own_s * col_n, own_t * row_n
    total_s, total_t = float(ns * row_n), float(nt * col_n)
    my_row, my_col = lax.axis_index("row"), lax.axis_index("col")
    col_peers = [lax.rem(my_col + k, col_n) for k in range(1, col_n)]
    row_peers = [lax.rem(my_row + k, row_n) for k in range(1, row_n)]

    barrier = pltpu.get_barrier_semaphore()
    for peer in col_peers:
        pl.semaphore_signal(barrier, inc=1, device_id={"col": peer}, device_id_type=MESH)
    for peer in row_peers:
        pl.semaphore_signal(barrier, inc=1, device_id={"row": peer}, device_id_type=MESH)
    pl.semaphore_wait(barrier, col_n + row_n - 2)

    s_rows = pl.ds(pl.multiple_of(my_col * own_s, own_s), own_s)
    t_rows = pl.ds(pl.multiple_of(my_row * own_t, own_t), own_t)
    gathers = []
    for k, peer in enumerate(row_peers):
        gathers.append(
            pltpu.make_async_remote_copy(
                t_ref, t_all.at[t_rows, :], t_send.at[k], t_recv.at[k],
                device_id={"row": peer}, device_id_type=MESH,
            )
        )
    for k, peer in enumerate(col_peers):
        gathers.append(
            pltpu.make_async_remote_copy(
                s_ref, s_all.at[s_rows, :], s_send.at[k], s_recv.at[k],
                device_id={"col": peer}, device_id_type=MESH,
            )
        )
    for copy in gathers:
        copy.start()
    s_all[s_rows, :] = s_ref[...]
    t_all[t_rows, :] = t_ref[...]
    for copy in gathers:
        copy.wait()

    chunk = min(512, own_s, own_t)
    lane = lax.broadcasted_iota(jnp.int32, (chunk, depth), 1)
    ones = jnp.where(lane < 3, 1.0, 0.0).astype(BF16)

    def s_prepare(i, _):
        rows = pl.ds(pl.multiple_of(i * chunk, chunk), chunk)
        x = s_all[rows, :].astype(F32)
        s_sq[:, rows] = jnp.sum(jnp.transpose(x * x), axis=0, keepdims=True)
        s_ext[rows, :] = ones
        return 0

    def t_prepare(i, _):
        rows = pl.ds(pl.multiple_of(i * chunk, chunk), chunk)
        x = t_all[rows, :].astype(F32)
        t_sq[:, rows] = jnp.sum(jnp.transpose(x * x), axis=0, keepdims=True)
        bias = jnp.sum(x * x, axis=1, keepdims=True) * -0.5
        t_ext[rows, :] = pick3(jnp.broadcast_to(bias, (chunk, depth)), lane, 0, 0.0)
        return 0

    lax.fori_loop(0, ns // chunk, s_prepare, 0)
    lax.fori_loop(0, nt // chunk, t_prepare, 0)

    def logs_pass(x_all, x_ext, w_all, w_ext, out, keep):
        nx, nw = x_all.shape[0], w_all.shape[0]
        width = z0.shape[1]
        tiles = nw // width
        step = min(512, nx)
        fine = min(64, step)

        def lanes(tile):
            return pl.ds(pl.multiple_of(tile * width, width), width)

        def scores(tile, q, z, highest):
            rows = pl.ds(q * step, step)
            at = lanes(tile)
            x = jnp.concatenate([x_all[rows, :], x_ext[rows, :]], axis=1)
            w = jnp.concatenate([w_all[at, :], w_ext[at, :]], axis=1)
            inner = nt_dot(x, w)
            z[rows, :] = inner
            return jnp.maximum(highest, jnp.max(inner.reshape(step // 8, 8, width), axis=0))

        def sums(tile, q, z, highest, summed):
            for j in range(q * step, (q + 1) * step, fine):
                rows = pl.ds(j, fine)
                shifted = z[rows, :].reshape(fine // 8, 8, width) - highest[None]
                terms = jnp.exp2(shifted * SCALE)
                if keep:
                    kept[rows, lanes(tile)] = terms.reshape(fine, width).astype(BF16)
                summed = summed + jnp.sum(terms, axis=0)
            return summed

        def settle(highest):
            return jnp.broadcast_to(jnp.max(highest, axis=0, keepdims=True), (8, width))

        low = jnp.full((8, width), -3e38, F32)

        def both(tile, z_now, highest, z_next):
            following = jnp.minimum(tile + 1, tiles - 1)
            new_high = low
            summed = jnp.zeros((8, width), F32)
            for q in range(nx // step):
                new_high = scores(following, q, z_next, new_high)
                summed = sums(tile, q, z_now, highest, summed)
            top = highest[0:1, :] * SCALE
            out[:, lanes(tile)] = top + log2(jnp.sum(summed, axis=0, keepdims=True))
            if keep:
                col_high[:, lanes(tile)] = top
            return settle(new_high)

        def pair(i, highest):
            highest = both(2 * i, z0, highest, z1)
            return both(2 * i + 1, z1, highest, z0)

        first = low
        for q in range(nx // step):
            first = scores(0, q, z0, first)
        lax.fori_loop(0, tiles // 2, pair, settle(first))

    def exchange(turn, sent, received, send, recv, axis, peers):
        copies = [
            pltpu.make_async_remote_copy(
                sent, received.at[turn, k], send.at[turn, k], recv.at[turn, k],
                device_id={axis: peer}, device_id_type=MESH,
            )
            for k, peer in enumerate(peers)
        ]
        for copy in copies:
            copy.start()
        for copy in copies:
            copy.wait()
        return [sent[...]] + [received[turn, k] for k in range(len(peers))]

    def over_col(turn):
        return exchange(turn, part.at[2 * turn], from_col, col_send, col_recv, "col", col_peers)

    def over_row(turn):
        return exchange(turn, part.at[2 * turn + 1], from_row, row_send, row_recv, "row", row_peers)

    def combined_logs(logs):
        highest = functools.reduce(jnp.maximum, logs)
        return highest + log2(sum(jnp.exp2(x - highest) for x in logs))

    logs_pass(t_all, t_ext, s_all, s_ext, part.at[0], False)
    f_first = math.log2(total_t) - combined_logs(over_col(0))
    f_ref[...] = f_first

    def s_bias(i, _):
        rows = pl.ds(pl.multiple_of(i * chunk, chunk), chunk)
        bias = jnp.transpose(jnp.broadcast_to(f_ref[:, rows] * (1.0 / SCALE), (depth, chunk)))
        s_ext[rows, :] = pick3(bias, lane, 0, 0.0)
        return 0

    def t_ones(i, _):
        t_ext[pl.ds(pl.multiple_of(i * chunk, chunk), chunk), :] = ones
        return 0

    lax.fori_loop(0, ns // chunk, s_bias, 0)
    lax.fori_loop(0, nt // chunk, t_ones, 0)
    logs_pass(s_all, s_ext, t_all, t_ext, part.at[1], True)
    g_first = math.log2(total_s) - combined_logs(over_row(0))
    g_ref[...] = g_first
    col_high[...] = jnp.exp2(g_first + col_high[...])

    block = min(512, ns, nt)

    def parts_of(x):
        index = lax.broadcasted_iota(jnp.int32, (16, x.shape[1]), 0)
        return pick3(jnp.broadcast_to(x, (16, x.shape[1])), index, 0, 0.0)

    def row_sums(x, out):
        lhs = parts_of(x)

        def one(i, _):
            rows = pl.ds(pl.multiple_of(i * block, block), block)
            out[:, rows] = jnp.sum(nt_dot(lhs, kept[rows, :]), axis=0, keepdims=True)
            return 0

        lax.fori_loop(0, ns // block, one, 0)

    def col_sums(x, out):
        lhs = parts_of(x)

        def one(i, _):
            at = pl.ds(pl.multiple_of(i * block, block), block)
            found = jnp.dot(lhs, kept[:, at], preferred_element_type=F32)
            out[:, at] = jnp.sum(found, axis=0, keepdims=True) * col_high[:, at]
            return 0

        lax.fori_loop(0, nt // block, one, 0)

    weight = col_high[...]
    for turn in range(1, ITERS):
        row_sums(weight, part.at[2 * turn])
        u = total_t / sum(over_col(turn))
        col_sums(u, part.at[2 * turn + 1])
        v = total_s / sum(over_row(turn))
        weight = col_high[...] * v
    f_ref[...] = BACK * (f_ref[...] + log2(u)) + s_sq[...]
    g_ref[...] = BACK * (g_ref[...] + log2(v)) + t_sq[...]


def careful(row_n, col_n, source, target):
    own_s, depth = source.shape
    own_t = target.shape[0]
    ns, nt = own_s * col_n, own_t * row_n
    width = min(256, ns // 2, nt // 2)
    vmem = pl.BlockSpec(memory_space=pltpu.VMEM)
    dma = pltpu.SemaphoreType.DMA
    f, g = pl.pallas_call(
        functools.partial(careful_kernel, row_n, col_n),
        out_shape=(jax.ShapeDtypeStruct((1, ns), F32), jax.ShapeDtypeStruct((1, nt), F32)),
        in_specs=[vmem, vmem],
        out_specs=(vmem, vmem),
        scratch_shapes=[
            pltpu.VMEM((ns, depth), BF16),
            pltpu.VMEM((nt, depth), BF16),
            pltpu.VMEM((ns, depth), BF16),
            pltpu.VMEM((nt, depth), BF16),
            pltpu.VMEM((ns, nt), BF16),
            pltpu.VMEM((max(ns, nt), width), F32),
            pltpu.VMEM((max(ns, nt), width), F32),
            pltpu.VMEM((2 * ITERS, 1, max(ns, nt)), F32),
            pltpu.VMEM((1, nt), F32),
            pltpu.VMEM((1, ns), F32),
            pltpu.VMEM((1, nt), F32),
            pltpu.VMEM((ITERS, col_n - 1, 1, ns), F32),
            pltpu.VMEM((ITERS, row_n - 1, 1, nt), F32),
            dma((col_n - 1,)),
            dma((col_n - 1,)),
            dma((row_n - 1,)),
            dma((row_n - 1,)),
            dma((ITERS, col_n - 1)),
            dma((ITERS, col_n - 1)),
            dma((ITERS, row_n - 1)),
            dma((ITERS, row_n - 1)),
        ],
        compiler_params=pltpu.CompilerParams(
            collective_id=1, has_side_effects=True, vmem_limit_bytes=60 << 20
        ),
        cost_estimate=pl.CostEstimate(
            flops=12 * ns * nt * depth, bytes_accessed=2 * (ns + nt) * depth, transcendentals=2 * ns * nt
        ),
    )(source, target)
    return f.reshape(ns), g.reshape(nt)


def on_device(row_n, col_n, source, target):
    own_s, depth = source.shape
    own_t = target.shape[0]
    ns, nt = own_s * col_n, own_t * row_n
    vmem = pl.BlockSpec(memory_space=pltpu.VMEM)
    dma = pltpu.SemaphoreType.DMA
    f, g = pl.pallas_call(
        functools.partial(kernel, row_n, col_n),
        out_shape=(jax.ShapeDtypeStruct((1, ns), F32), jax.ShapeDtypeStruct((1, nt), F32)),
        in_specs=[vmem, vmem],
        out_specs=(vmem, vmem),
        scratch_shapes=[
            pltpu.VMEM((ns, depth), BF16),
            pltpu.VMEM((nt, depth), BF16),
            pltpu.VMEM((ns, depth), BF16),
            pltpu.VMEM((nt, depth), BF16),
            pltpu.VMEM((ns, nt), BF16),
            pltpu.VMEM((8, ns), F32),
            pltpu.VMEM((8, nt), F32),
            pltpu.VMEM((nt, depth), F32),
            pltpu.VMEM((ns, 128), F32),
            pltpu.VMEM((1, nt), F32),
            pltpu.VMEM((2 * ITERS, 1, max(ns, nt)), F32),
            pltpu.VMEM((1, 1, nt), F32),
            pltpu.VMEM((1, ns), F32),
            pltpu.VMEM((1, nt), F32),
            pltpu.VMEM((1, ns), F32),
            pltpu.VMEM((1, nt), F32),
            pltpu.VMEM((own_t, 2 * depth), BF16),
            pltpu.VMEM((1, nt), F32),
            pltpu.VMEM((16, nt), BF16),
            pltpu.VMEM((ITERS, col_n - 1, 1, ns), F32),
            pltpu.VMEM((ITERS, row_n - 1, 1, nt), F32),
            dma((col_n // 2,)),
            dma((col_n // 2,)),
            dma((2, math.isqrt(row_n))),
            dma((2, math.isqrt(row_n))),
            dma((2 * math.isqrt(row_n),)),
            dma((2 * math.isqrt(row_n),)),
            dma((col_n // 2,)),
            dma((col_n // 2,)),
            dma((ITERS, 2, col_n - 1)),
            dma((ITERS, 2, col_n - 1)),
            dma((ITERS, 2, row_n - 1)),
            dma((ITERS, 2, row_n - 1)),
        ],
        compiler_params=pltpu.CompilerParams(
            collective_id=0, has_side_effects=True, vmem_limit_bytes=60 << 20
        ),
        cost_estimate=pl.CostEstimate(
            flops=12 * ns * nt * depth, bytes_accessed=2 * (ns + nt) * depth, transcendentals=2 * ns * nt
        ),
    )(source, target)
    fast = f.reshape(ns), g.reshape(nt)
    return lax.cond(jnp.isnan(f[0, 0]), lambda: careful(row_n, col_n, source, target), lambda: fast)


def solution(mesh):
    placed = (P(("row", "col"), None), P(("col", "row"), None))
    return jax.shard_map(
        functools.partial(on_device, mesh.shape["row"], mesh.shape["col"]),
        mesh=mesh,
        in_specs=placed,
        out_specs=(P("row"), P("col")),
        check_vma=False,
    )
```
